512 devices in a mesh: grp: 8 (over y, core), ep: 64 (over x, z).
Axes of the slice: x: 4, y: 4, z: 16, core: 2. Of those that a mesh axis runs over, the one named last changes fastest.
Arguments:
- tokens: bfloat16 [8192, 4096], P('ep'), may hold values from -6 to 6
- routes: int32 [8192, 8], P('ep'), may hold values from 0 to 127, all different within a row; in each aligned block of 128 rows (0 to 127, 128 to 255, ...) at most 10 rows name the same one
- route_weights: float32 [8192, 8], P('ep'), may hold values from 0.1 to 1
- expert_at_slot: int32 [64], replicated, may hold values from 0 to 127, as said below
- gate_up: bfloat16 [64, 4096, 2, 1024], P('ep', None, None, 'grp')
- down: bfloat16 [64, 1024, 4096], P('ep', 'grp'), may hold values from -0.1875 to 0.1875
Outputs:
- mixed: bfloat16 [8192, 4096], P('ep', 'grp')
- thresholds: float32 [64], replicated
The draws below stay inside these ranges and needn't reach their ends.
Inputs may be any that keep to these rules, and one draw needn't show every extreme that they name: `routes`: each row names 8 different experts. In the rows of one index of ep no expert is named by more than 10 rows, a bound that some block reaches. `expert_at_slot`: 64 different experts.
All inputs are finite; a program needn't handle non-finite values.
Results may differ from the reference program's by a relative error of at most 0.0057.
Values may be sent and summed in bfloat16 or wider, within the bound.
A program may use at most 64 MiB of HBM per device.

```python
import math
import jax
import jax.numpy as jnp
import numpy as np
from jax import lax

D = 4096
HID = 1024
EXPERTS_ALL = 128
TOPK = 8
NB = 128
TOK_DEV = 128
CAP = 10
SLOTS = 64
TOKENS = 8192
N_GRP = 8
N_EP = 64


def draw_expert_at_slot(key, part):
    key = jax.random.fold_in(key, 5)
    key_pick, key_order = jax.random.split(key)
    middle = 1 + jax.random.permutation(key_pick, EXPERTS_ALL - 2)[:SLOTS - 2].astype(jnp.int32)
    ends = jnp.array([0, EXPERTS_ALL - 1], jnp.int32)
    chosen = jnp.concatenate([ends, middle.astype(jnp.int32)])
    order = jax.random.permutation(key_order, SLOTS)
    return chosen[order].astype(jnp.int32)


def draw_gate_up(key, part):
    key = jax.random.fold_in(key, 11)
    key_entries, key_factor = jax.random.split(key)
    ramp_values = jnp.arange(HID, dtype=jnp.float32) / HID
    column = 0.5 * jnp.exp(jnp.log(4.0) * ramp_values)
    entries = jax.random.normal(key_entries, (SLOTS, D, 2, HID), jnp.float32)
    factor = jnp.exp(jax.random.uniform(key_factor, (SLOTS, 1, 2, HID), jnp.float32, -0.3, 0.3))
    return (entries * factor * column * D ** (-0.5)).astype(jnp.bfloat16)


def block_levels(stream_key, dims, cuts, least, largest):
    def one(dim, shards_of):
        steps = jax.random.uniform(jax.random.fold_in(jax.random.fold_in(stream_key, 6), dim), (shards_of,), jnp.float32, least / len(cuts), largest / len(cuts))
        return jnp.repeat(jnp.exp(steps), dims[dim] // shards_of).reshape((-1,) + (1,) * (len(dims) - dim - 1))

    loudness = one(*cuts[0])
    for cut in cuts[1:]:
        loudness = loudness * one(*cut)
    return loudness


def shared_out(key, own, number, rows, amount, top, reach, lean):
    sequence = jax.random.permutation(key, amount)
    crowded, ordinary = portions_of(amount, rows * top, reach, lean, True), portions_of(amount, rows * top, reach, lean, False)
    places = jnp.arange(amount)

    def named(lengths, offset_by):
        used = int((lengths > 0).sum())
        fixed = max(1, used // 4)
        shifted = fixed + (places - fixed + offset_by * (used - fixed)) % max(1, amount - fixed)
        return jnp.zeros((amount,), jnp.int32).at[sequence[jnp.where(places < fixed, places, shifted)]].set(jnp.asarray(lengths, jnp.int32))

    lengths = jnp.where(number % 4 == 0, named(crowded, number // 4), named(ordinary, number - number // 4 - 1))
    mixed = jax.random.permutation(jax.random.fold_in(own, 3), amount)
    giver, receiver = mixed[0:amount // 2 * 2:2], mixed[1:amount // 2 * 2:2]
    room = jnp.minimum(lengths[giver] - 1, reach - lengths[receiver]) // 2
    room = jnp.where((giver == sequence[0]) | (receiver == sequence[0]) | (lengths[receiver] == 0), 0, jnp.maximum(room, 0))
    shifted = jax.random.randint(jax.random.fold_in(own, 4), (amount // 2,), 0, 1 << 20) % (room + 1)
    lengths = lengths.at[giver].add(-shifted).at[receiver].add(shifted)
    items = jnp.searchsorted(jnp.cumsum(lengths), jnp.arange(rows * top), side="right").astype(jnp.int32)
    table = items.reshape(top, rows).T
    table = table[jax.random.permutation(jax.random.fold_in(own, 1), rows)]
    offset_by = jax.random.randint(jax.random.fold_in(own, 2), (rows, 1), 0, top)
    return jnp.take_along_axis(table, (jnp.arange(top)[None, :] + offset_by) % top, axis=1)


def portions_of(number_of, total, most, skew, full):
    loads = [(1 << 20) // math.isqrt(grade ** skew) + 1 for grade in range(1, number_of + 1)]
    largest = most if full else min(most, max(-(-total // number_of), total * loads[0] // sum(loads)))
    least = 1 if total - largest >= number_of - 1 else 0
    given, spare = [largest] + [least] * (number_of - 1), total - largest - least * (number_of - 1)
    while spare > 0:
        candidates = [i for i in range(1, number_of) if given[i] < largest] or [i for i in range(1, number_of) if given[i] < most]
        whole, left = sum([loads[i] for i in candidates]), spare
        for i in candidates:
            more = min(most - given[i], max(1, left * loads[i] // whole), spare)
            given[i] = given[i] + more
            spare = spare - more
    return np.array(given)


def scatter_about(own_key, extent, width, bound, cuts=(), kind=jnp.bfloat16):
    values = width * jax.random.normal(own_key, extent, jnp.float32)
    if cuts:
        values = values * block_levels(own_key, extent, cuts, -0.22, 0.18)
    return jnp.clip(values, -bound, bound).astype(kind)


def setup_inputs(seed: int = 0) -> dict:
    keys = jax.random.split(jax.random.key(seed), 7)
    tokens = scatter_about(keys[0], (TOKENS, D), 1.0, 6.0, ((0, 64),))
    routes_keys = jax.random.split(jax.random.fold_in(keys[1], 1), TOKENS // TOK_DEV)
    routes_turns = jax.random.permutation(jax.random.fold_in(keys[1], 3), TOKENS // TOK_DEV)
    routes = jax.vmap(lambda own, number: shared_out(jax.random.fold_in(keys[1], 2), own, number, TOK_DEV, EXPERTS_ALL, TOPK, CAP, 2))(routes_keys, routes_turns).reshape((TOKENS, TOPK))
    route_weights = jnp.clip(0.1 + 0.9 * jax.random.uniform(keys[2], (TOKENS, TOPK), jnp.float32) ** block_levels(keys[2], (TOKENS, TOPK), ((0, 64),), -0.2, 0.2), 0.1, 1.0)
    expert_at_slot = draw_expert_at_slot(jax.random.fold_in(keys[6], 71), 0)
    gate_up = draw_gate_up(jax.random.fold_in(keys[6], 71), 0)
    down = scatter_about(keys[5], (SLOTS, HID, D), HID ** -0.5, 0.1875, ((0, 64), (1, 8)))
    return dict(tokens=tokens, routes=routes, route_weights=route_weights, expert_at_slot=expert_at_slot, gate_up=gate_up, down=down)


hist_top = 16.0
quantile = 0.999


def soft_counts(values, row_weight, bin_count):
    width_bin = hist_top / bin_count
    magnitude = jnp.abs(values.astype(jnp.float32)).reshape(-1)
    weight_flat = jnp.broadcast_to(row_weight[:, None], values.shape).reshape(-1)
    block_size = math.gcd(magnitude.shape[0], 8192)
    centers = jnp.arange(bin_count, dtype=jnp.float32)

    def one_block(packed):
        levels, shares = packed
        position = jnp.clip(levels / width_bin - 0.5, 0.0, bin_count - 1.0)
        tent_weight = jnp.maximum(0.0, 1.0 - jnp.abs(position[:, None] - centers[None, :]))
        return jnp.sum(tent_weight * shares[:, None], axis=0)

    partials = lax.map(one_block, (magnitude.reshape(-1, block_size), weight_flat.reshape(-1, block_size)))
    return jnp.sum(partials, axis=0)


def clip_from(counts, bin_count):
    width_bin = hist_top / bin_count
    totals = jnp.sum(counts, axis=-1, keepdims=True)
    before = jnp.cumsum(counts, axis=-1) - counts
    fraction = jnp.clip((quantile * totals - before) / jnp.maximum(counts, 1.0), 0.0, 1.0)
    return width_bin * jnp.sum(fraction, axis=-1)


def reference(tokens, routes, route_weights, expert_at_slot, gate_up, down):
    kept_rows = N_EP * CAP
    slice_width = HID // N_GRP

    def per_slot(mixed_sum, slot_index):
        expert = expert_at_slot[slot_index]
        chosen = routes == expert
        member = jnp.any(chosen, axis=1)
        weight_row = jnp.sum(jnp.where(chosen, route_weights, 0.0), axis=1)
        row_order = jnp.argsort(1 - member.astype(jnp.int32), stable=True)[:kept_rows].astype(jnp.int32)
        row_valid = member[row_order].astype(jnp.float32)
        rows_in = tokens[row_order]
        weights_here = gate_up[slot_index]
        gate_sum = jnp.dot(rows_in, weights_here[:, 0, :], preferred_element_type=jnp.float32)
        lifted = jnp.dot(rows_in, weights_here[:, 1, :], preferred_element_type=jnp.float32)
        hidden = (jax.nn.silu(gate_sum) * lifted).astype(jnp.bfloat16)
        down_here = down[slot_index]
        expert_out = jnp.zeros((kept_rows, D), jnp.float32)
        for group_index in range(N_GRP):
            first_unit = group_index * slice_width
            partial_out = jnp.dot(hidden[:, first_unit:first_unit + slice_width], down_here[first_unit:first_unit + slice_width], preferred_element_type=jnp.float32)
            expert_out = expert_out + lax.optimization_barrier(partial_out.astype(jnp.bfloat16)).astype(jnp.float32)
        scaled = expert_out * (weight_row[row_order] * row_valid)[:, None]
        mixed_sum = mixed_sum.at[row_order].add(scaled)
        counts = soft_counts(hidden, row_valid, NB)
        return mixed_sum, counts

    start_sum = jnp.zeros((TOKENS, D), jnp.float32)
    mixed_sum, counts = lax.scan(per_slot, start_sum, jnp.arange(SLOTS, dtype=jnp.int32))
    return mixed_sum.astype(jnp.bfloat16), clip_from(counts, NB)
```

```python
import functools

import jax
import jax.numpy as jnp
import numpy as np
from jax import lax
from jax.experimental import pallas as pl
from jax.experimental.pallas import tpu as pltpu
from jax.sharding import PartitionSpec as P

NB = 128
CAP = 10
NY = 4
NC = 2
NX = 4
NZ = 16
HIST_TOP = 16.0
QUANTILE = 0.999
MESH = pl.DeviceIdType.MESH
F32 = jnp.float32
BF16 = jnp.bfloat16
HIGHEST = lax.Precision.HIGHEST
SEMS = 160


def dot(a, b, precision=None):
    return jnp.dot(a, b, preferred_element_type=F32, precision=precision)


def dot_nt(a, b):
    return lax.dot_general(a, b, (((1,), (1,)), ((), ())), preferred_element_type=F32)


def mask_bf16(m):
    return jnp.where(m, 1.0, 0.0).astype(BF16)


def iota(shape, dim):
    return lax.broadcasted_iota(jnp.int32, shape, dim)


def kernel(
    nx,
    nz,
    tokens,
    routes,
    route_weights,
    slots,
    gate_up,
    down,
    lane_info,
    perm_info,
    mixed,
    thresholds,
    tokz,
    meta,
    xsend,
    rows,
    w_raw,
    w_split,
    dn,
    acc,
    hid,
    outs,
    outr,
    zsend,
    zrecv,
    weights_hi,
    weights_lo,
    total,
    hist,
    valid_send,
    valid_recv,
    count_recv,
    th_send,
    th_recv,
    tx_send,
    tx_recv,
    send_sems,
    recv_sems,
    local_sems,
):
    ng = NY * NC
    per_group = nz // 2
    block_rows = per_group * CAP
    group_rows = nx * block_rows
    t_count = tokens.shape[0]
    feat = tokens.shape[1] // ng
    half_t = t_count // 2
    h_local = down.shape[0]

    g = lax.axis_index("grp")
    ep = lax.axis_index("ep")
    y, c = lax.div(g, NC), lax.rem(g, NC)
    x, z = lax.div(ep, nz), lax.rem(ep, nz)
    y_up, y_dn, y_op = lax.rem(y + 1, NY), lax.rem(y + NY - 1, NY), lax.rem(y + 2, NY)
    other = 1 - c
    z_up, z_dn = lax.rem(z + 1, nz), lax.rem(z + nz - 1, nz)

    def sl(j):
        return (j + nz // 4) % nz

    def at_z(zz):
        return (g, x * nz + zz)

    def at_x(xx):
        return (g, xx * nz + z)

    def at_g(gg):
        return (gg, ep)

    def g_of(yy, cc):
        return yy * NC + cc

    started = []
    used = [0]

    def send(src, dst, device):
        k = used[0]
        used[0] += 1
        copy = pltpu.make_async_remote_copy(
            src_ref=src,
            dst_ref=dst,
            send_sem=send_sems.at[k],
            recv_sem=recv_sems.at[k],
            device_id=device,
            device_id_type=MESH,
        )
        copy.start()
        started.append(copy)
        return k

    def arrived(k, ref):
        pltpu.make_async_remote_copy(
            src_ref=ref,
            dst_ref=ref,
            send_sem=send_sems.at[k],
            recv_sem=recv_sems.at[k],
            device_id=(g, ep),
            device_id_type=MESH,
        ).wait_recv()

    own = sl(0)
    take_tokens = pltpu.make_async_copy(
        tokens.at[:, pl.ds(pl.multiple_of(g * feat, 128), feat)], tokz.at[own], local_sems.at[0]
    )
    take_tokens.start()
    take_w = pltpu.make_async_copy(gate_up, w_raw, local_sems.at[1])
    take_w.start()
    take_down = pltpu.make_async_copy(
        down.at[:, pl.ds(pl.multiple_of(g * feat, 128), feat)], dn.at[g], local_sems.at[2]
    )
    take_down.start()

    barrier = pltpu.get_barrier_semaphore()
    peers = 0
    for j in range(1, nz):
        pl.semaphore_signal(barrier, inc=1, device_id=at_z(lax.rem(z + j, nz)), device_id_type=MESH)
        peers += 1
    for i in range(1, nx):
        pl.semaphore_signal(barrier, inc=1, device_id=at_x(lax.rem(x + i, nx)), device_id_type=MESH)
        peers += 1
    for q in range(1, ng):
        pl.semaphore_signal(barrier, inc=1, device_id=at_g(lax.rem(g + q, ng)), device_id_type=MESH)
        peers += 1

    picks = routes.shape[1]
    routes_f = routes[...].astype(F32).astype(BF16)
    spread = mask_bf16(iota((16, picks), 0) == iota((16, picks), 1))
    meta[own] = dot_nt(spread, routes_f).astype(BF16)

    pl.semaphore_wait(barrier, peers)
    take_tokens.wait()

    ring = {}

    def ring_send(s):
        for h in range(2):
            part = pl.ds(h * half_t, half_t)
            if s < nz // 2 or h == 0:
                ring["up", s, h] = send(
                    tokz.at[sl(s - 1), part], tokz.at[sl(s), part], at_z(z_up)
                )
            if s < nz // 2 or h == 1:
                ring["dn", s, h] = send(
                    tokz.at[sl(1 - s), part], tokz.at[sl(-s), part], at_z(z_dn)
                )
            if h == 0:
                ring["up", s] = send(meta.at[sl(s - 1)], meta.at[sl(s)], at_z(z_up))
                if s < nz // 2:
                    ring["dn", s] = send(meta.at[sl(1 - s)], meta.at[sl(-s)], at_z(z_dn))

    def ring_wait(s):
        for h in range(2):
            part = pl.ds(h * half_t, half_t)
            if s < nz // 2 or h == 0:
                arrived(ring["up", s, h], tokz.at[sl(s), part])
            if s < nz // 2 or h == 1:
                arrived(ring["dn", s, h], tokz.at[sl(-s), part])
        arrived(ring["up", s], meta.at[sl(s)])
        if s < nz // 2:
            arrived(ring["dn", s], meta.at[sl(-s)])

    tri = mask_bf16(iota((t_count, t_count), 0) < iota((t_count, t_count), 1))
    experts_here = jnp.full((8, 1), -1.0, F32)
    for i in range(nx):
        e = slots[lax.rem(x + i, nx) * nz + z].astype(F32)
        experts_here = jnp.where(iota((8, 1), 0) == i, e, experts_here)

    valid_sum = [jnp.zeros((8, t_count), F32)]
    x_keys = {}

    def select(grp_no):
        chosen = []
        for s in range(grp_no * per_group, (grp_no + 1) * per_group):
            table = meta[s].astype(F32)
            hit = jnp.zeros((8, t_count), F32)
            for k in range(picks):
                hit = jnp.maximum(hit, jnp.where(table[k : k + 1, :] == experts_here, 1.0, 0.0))
            valid_sum[0] = valid_sum[0] + hit
            chosen.append(hit)
        stacked = jnp.concatenate(chosen, axis=0)
        earlier = dot(stacked.astype(BF16), tri)
        first = lax.shift_right_logical(iota((8 * per_group, t_count), 0), 3) * CAP
        code = jnp.where(stacked > 0.5, earlier + first.astype(F32), -1.0)
        row = iota((block_rows, t_count), 0).astype(F32)
        values = tokz[grp_no * per_group : (grp_no + 1) * per_group].reshape(
            per_group * t_count, feat
        )
        for i in range(nx):
            sel = jnp.concatenate(
                [mask_bf16(row == code[8 * s + i : 8 * s + i + 1, :]) for s in range(per_group)],
                axis=1,
            )
            picked = dot(sel, values).astype(BF16)
            if i == 0:
                rows[g, grp_no, 0] = picked
            else:
                xsend[grp_no, i - 1] = picked
                x_keys[grp_no, i] = send(
                    xsend.at[grp_no, i - 1], rows.at[g, grp_no, i], at_x(lax.rem(x + i, nx))
                )

    def broadcast(ref):
        up, dn_, op = g_of(y_up, c), g_of(y_dn, c), g_of(y_op, c)
        mate = at_g(g_of(y, other))
        a_up = send(ref(g), ref(g), at_g(up))
        a_dn = send(ref(g), ref(g), at_g(dn_))
        a_mate = send(ref(g), ref(g), mate)
        yield
        arrived(a_up, ref(dn_))
        b_up = send(ref(dn_, 0), ref(dn_, 0), at_g(up))
        b_mate0 = send(ref(dn_), ref(dn_), mate)
        arrived(a_dn, ref(up))
        b_dn = send(ref(up, 1), ref(up, 1), at_g(dn_))
        b_mate1 = send(ref(up), ref(up), mate)
        yield
        arrived(b_up, ref(op, 0))
        c_mate0 = send(ref(op, 0), ref(op, 0), mate)
        arrived(b_dn, ref(op, 1))
        c_mate1 = send(ref(op, 1), ref(op, 1), mate)
        yield
        arrived(a_mate, ref(g_of(y, other)))
        arrived(b_mate0, ref(g_of(y_dn, other)))
        arrived(b_mate1, ref(g_of(y_up, other)))
        arrived(c_mate0, ref(g_of(y_op, other), 0))
        arrived(c_mate1, ref(g_of(y_op, other), 1))
        yield

    def rows_part(grp_no):
        def ref(q, half=None):
            if half is None:
                return rows.at[q, grp_no]
            return rows.at[q, grp_no, pl.ds(half * (nx // 2), nx // 2)]

        return ref

    def hid_part(grp_no):
        def ref(q, half=None):
            if half is None:
                return hid.at[q, grp_no]
            return hid.at[q, grp_no, pl.ds(half * (group_rows // 2), group_rows // 2)]

        return ref

    def x_arrived(grp_no):
        for i in range(1, nx):
            arrived(x_keys[grp_no, i], rows.at[g, grp_no, i])

    def gate_and_up(grp_no):
        acc[...] = jnp.zeros_like(acc)

        @pl.loop(0, ng)
        def _(q):
            block = rows[q, grp_no].reshape(group_rows, feat)
            acc[...] += dot(block, w_split[q])

        gate = acc[:, :h_local]
        hidden = gate / (1.0 + jnp.exp(-gate)) * acc[:, h_local:]
        hid[g, grp_no] = hidden.astype(BF16)

    def histogram(grp_no):
        wide = 16

        @pl.loop(0, group_rows // wide)
        def _(step):
            first = pl.multiple_of(step * wide, wide)
            level = jnp.abs(hid[g, grp_no, pl.ds(first, wide)].astype(F32))
            where = jnp.clip(level * (NB / HIST_TOP) - 0.5, 0.0, NB - 1.0)
            lower = jnp.floor(where)
            part = where - lower
            part_hi = part.astype(BF16).astype(F32)
            part_lo = part - part_hi
            coarse = jnp.floor(lower * (1.0 / 16.0))
            fine = lower - 16.0 * coarse
            eight = iota((8, h_local), 0).astype(F32)
            sixteen = iota((16, h_local), 0).astype(F32)
            left, one, high, low = [], [], [], []
            for r in range(wide):
                left.append(jnp.where(coarse[r : r + 1] == eight, 1.0, 0.0))
                match = fine[r : r + 1] == sixteen
                one.append(jnp.where(match, 1.0, 0.0))
                high.append(jnp.where(match, part_hi[r : r + 1], 0.0))
                low.append(jnp.where(match, part_lo[r : r + 1], 0.0))
            a = jnp.concatenate(left, axis=0).astype(BF16)
            b = jnp.concatenate(one + high + low, axis=0).astype(BF16)
            hist[...] += dot_nt(a, b)

    def counts_of():
        own_row = lax.shift_right_logical(iota((128, 256), 0), 3) == lax.shift_right_logical(
            iota((128, 256), 1), 4
        )
        fold = jnp.where((iota((256, NB), 0) & 15) == (iota((256, NB), 1) & 15), 1.0, 0.0)
        own_bin = (iota((128, NB), 0) & 7) == lax.shift_right_logical(iota((128, NB), 1), 4)

        def bins(table):
            folded = dot(jnp.where(own_row, table, 0.0), fold, HIGHEST)
            return jnp.sum(jnp.where(own_bin, folded, 0.0), axis=0, keepdims=True)

        number = bins(hist[:, :256])
        share = bins(hist[:, 256:512] + hist[:, 512:])
        share8 = jnp.broadcast_to(share, (8, NB))
        return jnp.broadcast_to(number, (8, NB)) - share8 + pltpu.roll(share8, 1, 1)

    def output_rows(grp_no):
        @pl.loop(0, nx)
        def _(i):
            first = pl.multiple_of(i * block_rows, 16)
            full_i = jnp.concatenate(
                [hid[q, grp_no, pl.ds(first, block_rows)] for q in range(ng)], axis=1
            )
            outs[grp_no, i] = dot(full_i, dn[...].reshape(ng * h_local, feat)).astype(BF16)

    o_keys = {}

    def x_return(grp_no):
        for i in range(1, nx):
            o_keys[grp_no, i] = send(
                outs.at[grp_no, i], outr.at[grp_no, i], at_x(lax.rem(x + nx - i, nx))
            )
        outr[grp_no, 0] = outs[grp_no, 0]

    z_keys = {}
    back_rows = 2 * nx * CAP
    half_f = feat // 2

    def z_return(grp_no):
        for i in range(1, nx):
            arrived(o_keys[grp_no, i], outr.at[grp_no, i])
        col = iota((back_rows, group_rows), 1)
        both = outr[grp_no].reshape(group_rows, feat)
        for k in range(per_group):
            s = grp_no * per_group + k
            upper = mask_bf16(col == perm_info[:, 0:1] + k * CAP)
            under = mask_bf16(col == perm_info[:, 1:2] + k * CAP)
            packed = (dot(upper, both[:, :half_f]) + dot(under, both[:, half_f:])).astype(BF16)
            j = (s - nz // 4) % nz
            if j == 0:
                zrecv[s] = packed
            else:
                zsend[s] = packed
                z_keys[s] = send(zsend.at[s], zrecv.at[s], at_z(lax.rem(z + nz - j, nz)))

    lanes = nz * back_rows

    def home_weights():
        chunk = 128
        index = lane_info[0:1, :]
        expert = jnp.full((1, lanes), -1, jnp.int32)
        for s in range(nz):
            j = (s - nz // 4) % nz
            for i in range(nx):
                e = slots[lax.rem(x + i, nx) * nz + lax.rem(z + j, nz)]
                expert = jnp.where(index == s * nx + i, e, expert)
        before = mask_bf16(iota((t_count, t_count), 1) < iota((t_count, t_count), 0))
        for q in range(0, lanes, chunk):
            part = slice(q, min(q + chunk, lanes))
            e = expert[:, part]
            hit = jnp.zeros((t_count, e.shape[1]), F32)
            weight = hit
            for k in range(picks):
                eq = routes[:, k : k + 1] == e
                hit = jnp.where(eq, 1.0, hit)
                weight = jnp.where(eq, route_weights[:, k : k + 1], weight)
            earlier = dot(before, hit.astype(BF16))
            place = lane_info[1:2, part].astype(F32)
            used_weight = jnp.where((hit > 0.5) & (earlier == place), weight, 0.0)
            top = used_weight.astype(BF16)
            weights_hi[:, part] = top
            weights_lo[:, part] = (used_weight - top.astype(F32)).astype(BF16)

    def combine(grp_no):
        width = per_group * back_rows
        part = slice(grp_no * width, (grp_no + 1) * width)
        back = zrecv[grp_no * per_group : (grp_no + 1) * per_group].reshape(width, half_f)
        for half in range(2):
            keep = lane_info[2:3, part] == half
            zero = jnp.zeros((), BF16)
            high = jnp.where(keep, weights_hi[:, part], zero)
            low = jnp.where(keep, weights_lo[:, part], zero)
            gained = dot(high, back) + dot(low, back)
            cols = slice(half * half_f, (half + 1) * half_f)
            if grp_no == 0:
                total[:, cols] = gained
            else:
                mixed[:, cols] = (total[:, cols] + gained).astype(BF16)

    def wait_back(grp_no):
        for k in range(per_group):
            s = grp_no * per_group + k
            if s in z_keys:
                arrived(z_keys[s], zrecv.at[s])

    def split_weights():
        take_w.wait()
        size = 2 * 128
        r, q = iota((size, size), 0), iota((size, size), 1)
        source = jnp.where(r < 128, 2 * r, 2 * (r - 128) + 1)
        order = mask_bf16(q == source)
        per = feat // 128

        @pl.loop(0, ng)
        def _(gg):
            for b in range(per):
                first = pl.multiple_of((gg * per + b) * size, size)
                mixed_up = dot(order, w_raw[pl.ds(first, size)]).astype(BF16)
                w_split[gg, b * 128 : (b + 1) * 128, :h_local] = mixed_up[:128]
                w_split[gg, b * 128 : (b + 1) * 128, h_local:] = mixed_up[128:]

    down_keys = []

    def send_down():
        for q in range(1, ng):
            to = lax.rem(g + q, ng)
            columns = pl.ds(pl.multiple_of(to * feat, 128), feat)
            down_keys.append(send(down.at[:, columns], dn.at[g], at_g(to)))

    rows_a, rows_b = None, None

    ring_send(1)
    send_down()
    hist[...] = jnp.zeros_like(hist)
    split_weights()
    bcast = {}

    def start_rows(grp_no):
        x_arrived(grp_no)
        bcast[grp_no] = broadcast(rows_part(grp_no))
        next(bcast[grp_no])

    stages = [
        lambda: select(0),
        lambda: start_rows(0),
        lambda: next(bcast[0]),
        lambda: next(bcast[0]),
    ]
    for s in range(2, nz // 2 + 1):
        ring_wait(s - 1)
        ring_send(s)
        if s == 2:
            home_weights()
        if s > nz // 4 and stages:
            stages.pop(0)()
    ring_wait(nz // 2)
    select(1)
    for stage in stages:
        stage()

    number = jnp.broadcast_to(jnp.sum(valid_sum[0], axis=1, keepdims=True), (8, 128))
    valid_keys = {}
    for i in range(nx):
        line = jnp.broadcast_to(number[i : i + 1, :], (8, 128))
        if i == 0:
            valid_recv[0] = line
        else:
            valid_send[i - 1] = line
            valid_keys[i] = send(
                valid_send.at[i - 1], valid_recv.at[i], at_x(lax.rem(x + i, nx))
            )

    next(bcast[0])
    gate_and_up(0)
    hidden_a = broadcast(hid_part(0))
    next(hidden_a)
    start_rows(1)
    next(hidden_a)
    next(bcast[1])
    histogram(0)
    next(hidden_a)
    take_down.wait()
    for q in range(1, ng):
        arrived(down_keys[q - 1], dn.at[lax.rem(g + ng - q, ng)])
    next(hidden_a)
    output_rows(0)
    x_return(0)
    next(bcast[1])
    next(bcast[1])
    gate_and_up(1)
    hidden_b = broadcast(hid_part(1))
    next(hidden_b)
    z_return(0)
    next(hidden_b)
    histogram(1)
    counts = counts_of()
    filled = valid_recv[0]
    for i in range(1, nx):
        arrived(valid_keys[i], valid_recv.at[i])
        filled = filled + valid_recv[i]
    empty = (float(2 * group_rows) - filled) * float(h_local)
    counts = counts - jnp.where(iota((8, NB), 1) == 0, empty, 0.0)
    count_recv[g] = counts
    count_keys = {}
    for q in range(1, ng):
        count_keys[q] = send(count_recv.at[g], count_recv.at[g], at_g(lax.rem(g + q, ng)))
    next(hidden_b)
    next(hidden_b)
    output_rows(1)
    x_return(1)

    for q in range(1, ng):
        from_g = lax.rem(g + ng - q, ng)
        arrived(count_keys[q], count_recv.at[from_g])
    counts = count_recv[0]
    for q in range(1, ng):
        counts = counts + count_recv[q]
    sums = jnp.sum(counts, axis=1, keepdims=True)
    below = jnp.where(iota((NB, NB), 0) < iota((NB, NB), 1), 1.0, 0.0)
    before_bin = dot(counts, below, HIGHEST)
    fraction = jnp.clip((QUANTILE * sums - before_bin) / jnp.maximum(counts, 1.0), 0.0, 1.0)
    threshold = (HIST_TOP / NB) * jnp.sum(fraction, axis=1, keepdims=True)
    th_send[...] = jnp.broadcast_to(threshold, (8, 128))
    th_recv[0] = th_send[...]
    th_keys = {}
    for j in range(1, nz):
        th_keys[j] = send(th_send, th_recv.at[j], at_z(lax.rem(z + j, nz)))
    z_return(1)
    gathered = jnp.zeros((8, 128), F32)
    for j in range(nz):
        if j:
            arrived(th_keys[j], th_recv.at[j])
        place = x * nz + lax.rem(z + nz - j, nz)
        gathered = jnp.where(iota((8, 128), 1) == place, th_recv[j], gathered)
    tx_send[...] = gathered
    tx_keys = {}
    for i in range(1, nx):
        tx_keys[i] = send(tx_send, tx_recv.at[i - 1], at_x(lax.rem(x + i, nx)))

    wait_back(0)
    combine(0)
    for i in range(1, nx):
        arrived(tx_keys[i], tx_recv.at[i - 1])
        gathered = gathered + tx_recv[i - 1]
    thresholds[...] = gathered
    wait_back(1)
    combine(1)
    for copy in started:
        copy.wait_send()


def per_device(nx, nz, tokens, routes, route_weights, slots, gate_up, down):
    ng = NY * NC
    t_count, width = tokens.shape
    feat = width // ng
    h_local = down.shape[1]
    per_group = nz // 2
    block_rows = per_group * CAP
    group_rows = nx * block_rows
    back_rows = 2 * nx * CAP
    lanes = nz * back_rows

    lane = np.arange(lanes)
    in_plane = lane % back_rows
    entry = in_plane % (nx * CAP)
    lane_info = np.zeros((8, lanes), np.int32)
    lane_info[0] = lane // back_rows * nx + entry // CAP
    lane_info[1] = entry % CAP
    lane_info[2] = in_plane // (nx * CAP)
    r = np.arange(back_rows)
    source = r % (nx * CAP) // CAP * block_rows + r % CAP
    perm_info = np.full((back_rows, 128), -(1 << 20), np.int32)
    perm_info[: nx * CAP, 0] = source[: nx * CAP]
    perm_info[nx * CAP :, 1] = source[nx * CAP :]

    vmem = pl.BlockSpec(memory_space=pltpu.VMEM)
    hbm = pl.BlockSpec(memory_space=pl.ANY)
    smem = pl.BlockSpec(memory_space=pltpu.SMEM)
    mixed, thresholds = pl.pallas_call(
        functools.partial(kernel, nx, nz),
        out_shape=(
            jax.ShapeDtypeStruct((t_count, feat), BF16),
            jax.ShapeDtypeStruct((8, 128), F32),
        ),
        in_specs=[hbm, vmem, vmem, smem, hbm, hbm, vmem, vmem],
        out_specs=(vmem, vmem),
        scratch_shapes=[
            pltpu.VMEM((nz, t_count, feat), BF16),
            pltpu.VMEM((nz, 16, t_count), BF16),
            pltpu.VMEM((2, nx - 1, block_rows, feat), BF16),
            pltpu.VMEM((ng, 2, nx, block_rows, feat), BF16),
            pltpu.VMEM((2 * width, h_local), BF16),
            pltpu.VMEM((ng, feat, 2 * h_local), BF16),
            pltpu.VMEM((ng, h_local, feat), BF16),
            pltpu.VMEM((group_rows, 2 * h_local), F32),
            pltpu.VMEM((ng, 2, group_rows, h_local), BF16),
            pltpu.VMEM((2, nx, block_rows, feat), BF16),
            pltpu.VMEM((2, nx, block_rows, feat), BF16),
            pltpu.VMEM((nz, back_rows, feat // 2), BF16),
            pltpu.VMEM((nz, back_rows, feat // 2), BF16),
            pltpu.VMEM((t_count, lanes), BF16),
            pltpu.VMEM((t_count, lanes), BF16),
            pltpu.VMEM((t_count, feat), F32),
            pltpu.VMEM((128, 768), F32),
            pltpu.VMEM((nx - 1, 8, 128), F32),
            pltpu.VMEM((nx, 8, 128), F32),
            pltpu.VMEM((ng, 8, 128), F32),
            pltpu.VMEM((8, 128), F32),
            pltpu.VMEM((nz, 8, 128), F32),
            pltpu.VMEM((8, 128), F32),
            pltpu.VMEM((nx - 1, 8, 128), F32),
            pltpu.SemaphoreType.DMA((SEMS,)),
            pltpu.SemaphoreType.DMA((SEMS,)),
            pltpu.SemaphoreType.DMA((3,)),
        ],
        compiler_params=pltpu.CompilerParams(
            collective_id=0, has_side_effects=True, vmem_limit_bytes=50 << 20
        ),
        cost_estimate=pl.CostEstimate(flops=4 << 30, bytes_accessed=8 << 20, transcendentals=1 << 17),
    )(
        tokens,
        routes,
        route_weights,
        slots,
        gate_up.reshape(2 * width, h_local),
        down[0],
        jnp.asarray(lane_info),
        jnp.asarray(perm_info),
    )
    return mixed, thresholds[0, : slots.shape[0]]


def solution(mesh, nx=NX, nz=NZ):
    placed = (
        P("ep", None),
        P("ep", None),
        P("ep", None),
        P(),
        P("ep", None, None, "grp"),
        P("ep", "grp", None),
    )
    return jax.shard_map(
        functools.partial(per_device, nx, nz),
        mesh=mesh,
        in_specs=placed,
        out_specs=(P("ep", "grp"), P()),
        check_vma=False,
    )
```

```python
import functools

import jax
import jax.numpy as jnp
from jax import lax
from jax.experimental import pallas as pl
from jax.experimental.pallas import tpu as pltpu
from jax.sharding import PartitionSpec as P

NB = 128
CAP = 10
NY = 4
NC = 2
NX = 4
NZ = 16
NQ = 4
HIST_TOP = 16.0
QUANTILE = 0.999
MESH = pl.DeviceIdType.MESH
F32 = jnp.float32
BF16 = jnp.bfloat16
HIGHEST = lax.Precision.HIGHEST
SEMS = 220
FIRST = 12.0
SPACING = 7.0
AFTER = (0.0, 4.7, 11.0, 15.5, 16.8, 22.0, 23.1, 28.5)


def dot(a, b, precision=None):
    return jnp.dot(a, b, preferred_element_type=F32, precision=precision)


def dot_nt(a, b, precision=None):
    return lax.dot_general(
        a, b, (((1,), (1,)), ((), ())), preferred_element_type=F32, precision=precision
    )


def mask_f32(m):
    return jnp.where(m, 1.0, 0.0)


def mask_bf16(m):
    return mask_f32(m).astype(BF16)


def iota(shape, dim):
    return lax.broadcasted_iota(jnp.int32, shape, dim)


def split(value, by):
    whole = jnp.floor((value + 0.5) * (1.0 / by))
    return whole, value - whole * by


def kernel(
    nx,
    nz,
    tokens,
    routes_t,
    weights_t,
    slots_hbm,
    gate_up,
    down,
    mixed,
    thresholds,
    slots,
    routes_v,
    weights_v,
    own_tokens,
    fwd_send,
    fwd,
    xsend,
    rows,
    w_raw,
    w_split,
    dn,
    acc,
    hid,
    outs,
    outr,
    zsend,
    zrecv,
    perm_in,
    perm_out,
    weights_hi,
    weights_lo,
    total,
    hist,
    plane_send,
    plane_recv,
    valid_send,
    valid_recv,
    count_recv,
    th_send,
    th_recv,
    tx_send,
    tx_recv,
    send_sems,
    recv_sems,
    local_sems,
):
    ng = NY * NC
    planes = nz // NQ
    part_rows = planes * CAP
    quarter_rows = nx * part_rows
    t_count = tokens.shape[0]
    feat = tokens.shape[1] // ng
    half_f = feat // 2
    h_local = down.shape[0]
    picks = routes_t.shape[0]
    back_rows = 2 * nx * CAP

    g = lax.axis_index("grp")
    ep = lax.axis_index("ep")
    y, c = lax.div(g, NC), lax.rem(g, NC)
    x, z = lax.div(ep, nz), lax.rem(ep, nz)
    other = 1 - c

    def g_of(yy, cc):
        return yy * NC + cc

    g_up = g_of(lax.rem(y + 1, NY), c)
    g_dn = g_of(lax.rem(y + NY - 1, NY), c)
    g_op = g_of(lax.rem(y + 2, NY), c)
    g_mate = g_of(y, other)

    def mate_of(q):
        return q + other - c

    offsets = []
    for n in range(NQ - 1):
        offsets += [nz // 2 - 1 - n, n + 1 - nz // 2, n + 1, -1 - n]
    offsets += [nz // 4, -(nz // 4), nz // 2, 0]
    if planes == 1:
        offsets = [1, -1, 2, 0]

    def offset(s):
        return offsets[s]

    def plane(j):
        return lax.rem(z + j + nz, nz)

    def at_z(zz):
        return (g, x * nz + zz)

    def at_x(xx):
        return (g, xx * nz + z)

    def at_g(gg):
        return (gg, ep)

    started = []
    used = [0]

    def send(src, dst, device):
        k = used[0]
        used[0] += 1
        copy = pltpu.make_async_remote_copy(
            src_ref=src,
            dst_ref=dst,
            send_sem=send_sems.at[k],
            recv_sem=recv_sems.at[k],
            device_id=device,
            device_id_type=MESH,
        )
        copy.start()
        started.append(copy)
        return k

    def arrived(k, ref):
        pltpu.make_async_remote_copy(
            src_ref=ref,
            dst_ref=ref,
            send_sem=send_sems.at[k],
            recv_sem=recv_sems.at[k],
            device_id=(g, ep),
            device_id_type=MESH,
        ).wait_recv()

    def take(src, dst, k):
        copy = pltpu.make_async_copy(src, dst, local_sems.at[k])
        copy.start()
        return copy

    mine = pl.ds(pl.multiple_of(g * feat, 128), feat)
    take_routes = take(routes_t, routes_v, 0)
    take_tokens = take(tokens.at[:, mine], own_tokens, 1)
    take_slots = take(slots_hbm, slots, 2)
    take_weights = take(weights_t, weights_v, 3)
    take_w = take(gate_up, w_raw, 4)
    take_down = take(down.at[:, mine], dn.at[g], 5)

    barrier = pltpu.get_barrier_semaphore()
    peers = (
        [at_z(lax.rem(z + j, nz)) for j in range(1, nz)]
        + [at_x(lax.rem(x + i, nx)) for i in range(1, nx)]
        + [at_g(lax.rem(g + q, ng)) for q in range(1, ng)]
    )
    for peer in peers:
        pl.semaphore_signal(barrier, inc=1, device_id=peer, device_id_type=MESH)

    take_routes.wait()
    take_slots.wait()
    routes_f = routes_v[...].astype(F32)
    lines = nz * nx
    experts = jnp.full((lines, 1), -1.0, F32)
    for s in range(nz):
        for i in range(nx):
            e = slots[lax.rem(x + i, nx) * nz + plane(offset(s))].astype(F32)
            experts = jnp.where(iota((lines, 1), 0) == s * nx + i, e, experts)
    chosen = jnp.zeros((lines, t_count), F32)
    for k in range(picks):
        chosen = jnp.where(routes_f[k : k + 1, :] == experts, 1.0, chosen)
    tri = mask_bf16(iota((t_count, t_count), 0) < iota((t_count, t_count), 1))
    earlier = dot(chosen.astype(BF16), tri)
    code = jnp.where(chosen > 0.5, earlier, -100.0)
    number = jnp.sum(chosen, axis=1, keepdims=True)
    for s in range(nz):
        for i in range(nx):
            line = jnp.broadcast_to(number[s * nx + i : s * nx + i + 1, :], (1, 128))
            plane_send[s, i : i + 1, :] = line
        plane_send[s, nx:8, :] = jnp.zeros((8 - nx, 128), F32)

    def pack(value):
        return jnp.concatenate([value[:, :half_f], value[:, half_f:]], axis=0).astype(BF16)

    take_tokens.wait()
    row = iota((nx * CAP, t_count), 0).astype(F32)
    keys = {}

    def dispatch(n):
        sel = []
        for s in range(n * planes, (n + 1) * planes):
            wanted = jnp.zeros((nx * CAP, t_count), F32)
            for i in range(nx):
                place = code[s * nx + i : s * nx + i + 1, :] + float(i * CAP)
                wanted = jnp.where(row == place, 1.0, wanted)
            sel.append(wanted)
        picked = dot(jnp.concatenate(sel, axis=0).astype(BF16), own_tokens[...])
        for k in range(planes):
            s = n * planes + k
            packed = pack(picked[k * nx * CAP : (k + 1) * nx * CAP])
            if offset(s) == 0:
                fwd[s] = packed
            else:
                fwd_send[s] = packed

    def dispatch_send(n):
        for s in range(n * planes, (n + 1) * planes):
            if offset(s):
                to = at_z(plane(offset(s)))
                keys["fwd", s] = send(fwd_send.at[s], fwd.at[s], to)

    dispatch(0)
    pl.semaphore_wait(barrier, len(peers))
    for s in range(nz):
        if offset(s) == 0:
            plane_recv[s] = plane_send[s]
        else:
            keys["plane", s] = send(plane_send.at[s], plane_recv.at[s], at_z(plane(offset(s))))
    dispatch_send(0)
    for n in range(1, NQ):
        dispatch(n)
        dispatch_send(n)
    down_keys = []
    for q in range(1, ng):
        to = lax.rem(g + q, ng)
        columns = pl.ds(pl.multiple_of(to * feat, 128), feat)
        down_keys.append(send(down.at[:, columns], dn.at[g], at_g(to)))

    hist[...] = jnp.zeros_like(hist)

    def swap(a, b):
        row = iota((2 * quarter_rows, 1), 0).astype(F32)
        j, row = split(row, 2 * a * CAP)
        half, row = split(row, a * CAP)
        i, p = split(row, CAP)
        source = i * (2.0 * b * CAP) + half * (b * CAP) + j * CAP + p
        return mask_bf16(iota((2 * quarter_rows, 2 * quarter_rows), 1).astype(F32) == source)

    size = 2 * quarter_rows
    perm_in[...] = swap(planes, nx)
    perm_out[...] = swap(nx, planes)

    def split_weights():
        take_w.wait()
        wide = 2 * 128
        r, q = iota((wide, wide), 0), iota((wide, wide), 1)
        order = mask_bf16(q == jnp.where(r < 128, 2 * r, 2 * (r - 128) + 1))
        per = feat // 128

        @pl.loop(0, ng)
        def _(gg):
            for b in range(per):
                first = pl.multiple_of((gg * per + b) * wide, wide)
                parted = dot(order, w_raw[pl.ds(first, wide)]).astype(BF16)
                half, b = b * 128 // half_f, b * 128 % half_f
                to = 2 * h_local * half
                w_split[gg, b : b + 128, to : to + h_local] = parted[:128]
                w_split[gg, b : b + 128, to + h_local : to + 2 * h_local] = parted[128:]

    def home_weights():
        take_weights.wait()
        eye = mask_f32(iota((t_count, t_count), 0) == iota((t_count, t_count), 1))
        routes_c = dot_nt(eye, routes_v[...].astype(F32), HIGHEST)
        weights_c = dot_nt(eye, weights_v[...], HIGHEST)
        before = mask_bf16(iota((t_count, t_count), 1) < iota((t_count, t_count), 0))
        lane_k, in_plane = split(iota((1, size), 1).astype(F32), back_rows)
        _, entry = split(in_plane, nx * CAP)
        lane_i, place = split(entry, CAP)
        for quarter in range(NQ):
            expert = jnp.full((1, size), -1.0, F32)
            for k in range(planes):
                j = offset(quarter * planes + k)
                for i in range(nx):
                    e = slots[lax.rem(x + i, nx) * nz + plane(j)].astype(F32)
                    expert = jnp.where((lane_k == k) & (lane_i == i), e, expert)
            hit = jnp.zeros((t_count, size), F32)
            weight = hit
            for k in range(picks):
                eq = routes_c[:, k : k + 1] == expert
                hit = jnp.where(eq, 1.0, hit)
                weight = jnp.where(eq, weights_c[:, k : k + 1], weight)
            earlier = dot(before, hit.astype(BF16))
            weight = jnp.where((hit > 0.5) & (earlier == place), weight, 0.0)
            top = weight.astype(BF16)
            weights_hi[quarter] = top
            weights_lo[quarter] = (weight - top.astype(F32)).astype(BF16)

    def select(n):
        for s in range(n * planes, (n + 1) * planes):
            if offset(s):
                arrived(keys["fwd", s], fwd.at[s])
        block = fwd[n * planes : (n + 1) * planes].reshape(size, half_f)
        moved = dot(perm_in[...], block).astype(BF16)
        for i in range(nx):
            part = moved[i * 2 * part_rows : (i + 1) * 2 * part_rows]
            if i == 0:
                rows[g, n, 0] = part
            else:
                xsend[n, i - 1] = part
                keys["x", n, i] = send(
                    xsend.at[n, i - 1], rows.at[g, n, i], at_x(lax.rem(x + i, nx))
                )

    def rows_1(n):
        for i in range(1, nx):
            arrived(keys["x", n, i], rows.at[g, n, i])
        own = rows.at[g, n]
        keys["r_up", n] = send(own, own, at_g(g_up))
        keys["r_dn", n] = send(own, own, at_g(g_dn))
        keys["r_mate", n] = send(own, own, at_g(g_mate))

    near, far = pl.ds(0, nx // 2), pl.ds(nx // 2, nx // 2)

    def rows_2(n):
        ref = rows.at[g_dn, n]
        arrived(keys["r_up", n], ref)
        keys["r_up2", n] = send(rows.at[g_dn, n, near], rows.at[g_dn, n, near], at_g(g_up))
        keys["m_dn", n] = send(ref, ref, at_g(g_mate))
        ref = rows.at[g_up, n]
        arrived(keys["r_dn", n], ref)
        keys["r_dn2", n] = send(rows.at[g_up, n, far], rows.at[g_up, n, far], at_g(g_dn))
        keys["m_up", n] = send(ref, ref, at_g(g_mate))

    def rows_3(n):
        ref = rows.at[g_op, n, near]
        arrived(keys["r_up2", n], ref)
        keys["m_op1", n] = send(ref, ref, at_g(g_mate))
        ref = rows.at[g_op, n, far]
        arrived(keys["r_dn2", n], ref)
        keys["m_op2", n] = send(ref, ref, at_g(g_mate))
        gate_and_up(n, c)

    def rows_4(n):
        arrived(keys["r_mate", n], rows.at[g_mate, n])
        arrived(keys["m_dn", n], rows.at[mate_of(g_dn), n])
        arrived(keys["m_up", n], rows.at[mate_of(g_up), n])
        arrived(keys["m_op1", n], rows.at[mate_of(g_op), n, near])
        arrived(keys["m_op2", n], rows.at[mate_of(g_op), n, far])
        gate_and_up(n, other)
        activate(n)
        own = hid.at[g, n]
        for name, to in (("up", g_up), ("dn", g_dn), ("op", g_op), ("mate", g_mate)):
            keys["h_" + name, n] = send(own, own, at_g(to))
        histogram(n)
        if n == NQ - 1:
            send_counts()

    def hid_2(n):
        for name, src in (("up", g_dn), ("dn", g_up), ("op", g_op)):
            ref = hid.at[src, n]
            arrived(keys["h_" + name, n], ref)
            keys["hm_" + name, n] = send(ref, ref, at_g(g_mate))

    def hid_3(n):
        if n == 0:
            take_down.wait()
            for q in range(1, ng):
                arrived(down_keys[q - 1], dn.at[lax.rem(g + ng - q, ng)])
        arrived(keys["h_mate", n], hid.at[g_mate, n])
        for name, src in (("up", g_dn), ("dn", g_up), ("op", g_op)):
            arrived(keys["hm_" + name, n], hid.at[mate_of(src), n])
        output_rows(n)
        if n == NQ - 1:
            send_threshold()

    def gate_and_up(n, core):
        if n not in begun:
            begun.append(n)
            acc[n] = jnp.zeros((size, 4 * h_local), F32)

        @pl.loop(0, NY)
        def _(yy):
            q = g_of(yy, core)
            acc[n] += dot(rows[q, n].reshape(size, half_f), w_split[q])

    begun = []

    def activate(n):
        both = []
        for i in range(nx):
            r = 2 * part_rows * i
            both.append(
                acc[n, r : r + part_rows, : 2 * h_local]
                + acc[n, r + part_rows : r + 2 * part_rows, 2 * h_local :]
            )
        both = jnp.concatenate(both, axis=0)
        gate = both[:, :h_local]
        hid[g, n] = (gate / (1.0 + jnp.exp(-gate)) * both[:, h_local:]).astype(BF16)

    wide = hist.shape[0] // 8

    def histogram(n):
        @pl.loop(0, quarter_rows // (2 * wide))
        def _(step):
            first = pl.multiple_of(step * 2 * wide, 2 * wide)
            level = jnp.abs(hid[g, n, pl.ds(first, 2 * wide)].astype(F32))
            where = jnp.clip(level * (NB / HIST_TOP) - 0.5, 0.0, NB - 1.0)
            lower = jnp.floor(where)
            part = where - lower
            coarse = jnp.floor(lower * (1.0 / 16.0))
            fine = lower - 16.0 * coarse
            eight = iota((8, h_local), 0).astype(F32)
            sixteen = iota((16, h_local), 0).astype(F32)
            sides = []
            for side in range(2):
                left, one, share = [], [], []
                for r in range(side * wide, (side + 1) * wide):
                    left.append(mask_f32(coarse[r : r + 1] == eight))
                    match = fine[r : r + 1] == sixteen
                    one.append(mask_f32(match))
                    share.append(jnp.where(match, part[r : r + 1], 0.0))
                sides.append(
                    (
                        jnp.concatenate(left, axis=0).astype(BF16),
                        jnp.concatenate(one + share, axis=0).astype(BF16),
                    )
                )
            a = jnp.concatenate([sides[0][0], sides[1][0]], axis=1)
            b = jnp.concatenate([sides[0][1], sides[1][1]], axis=1)
            hist[...] += dot_nt(a, b)

    def counts_of():
        m, k = 8 * wide, 16 * wide
        own_row = lax.shift_right_logical(iota((m, k), 0), 3) == lax.shift_right_logical(
            iota((m, k), 1), 4
        )
        fold = mask_f32((iota((k, NB), 0) & 15) == (iota((k, NB), 1) & 15))
        own_bin = (iota((m, NB), 0) & 7) == lax.shift_right_logical(iota((m, NB), 1), 4)

        def bins(table):
            folded = dot(jnp.where(own_row, table, 0.0), fold, HIGHEST)
            return jnp.sum(jnp.where(own_bin, folded, 0.0), axis=0, keepdims=True)

        number = bins(hist[:, :k])
        share = jnp.broadcast_to(bins(hist[:, k:]), (8, NB))
        return jnp.broadcast_to(number, (8, NB)) - share + pltpu.roll(share, 1, 1)

    def output_rows(n):
        full = jnp.concatenate([hid[q, n] for q in range(ng)], axis=1)
        made = dot(full, dn[...].reshape(ng * h_local, feat))
        for i in range(nx):
            packed = pack(made[i * part_rows : (i + 1) * part_rows])
            if i == 0:
                outr[n, 0] = packed
            else:
                outs[n, i - 1] = packed
                keys["out", n, i] = send(
                    outs.at[n, i - 1], outr.at[n, i], at_x(lax.rem(x + nx - i, nx))
                )

    def z_return(n):
        for i in range(1, nx):
            arrived(keys["out", n, i], outr.at[n, i])
        moved = dot(perm_out[...], outr[n].reshape(size, half_f)).astype(BF16)
        for k in range(planes):
            s = n * planes + k
            block = moved[k * back_rows : (k + 1) * back_rows]
            j = offset(s)
            if j == 0:
                zrecv[s] = block
            else:
                zsend[s] = block
                keys["back", s] = send(zsend.at[s], zrecv.at[s], at_z(plane(-j)))

    def combine(n):
        for s in range(n * planes, (n + 1) * planes):
            if offset(s):
                arrived(keys["back", s], zrecv.at[s])
        back = zrecv[n * planes : (n + 1) * planes].reshape(size, half_f)
        _, in_plane = split(iota((1, size), 1).astype(F32), back_rows)
        upper = in_plane < nx * CAP
        zero = jnp.zeros((), BF16)
        for half in range(2):
            keep = upper if half == 0 else jnp.logical_not(upper)
            high = jnp.where(keep, weights_hi[n], zero)
            low = jnp.where(keep, weights_lo[n], zero)
            gained = dot(high, back) + dot(low, back)
            cols = slice(half * half_f, (half + 1) * half_f)
            if n > 0:
                gained = total[:, cols] + gained
            if n < NQ - 1:
                total[:, cols] = gained
            else:
                mixed[:, cols] = gained.astype(BF16)

    def send_valid():
        number = jnp.zeros((8, 128), F32)
        for s in range(nz):
            if offset(s):
                arrived(keys["plane", s], plane_recv.at[s])
            number = number + plane_recv[s]
        for i in range(nx):
            line = jnp.broadcast_to(number[i : i + 1, :], (8, 128))
            if i == 0:
                valid_recv[0] = line
            else:
                valid_send[i - 1] = line
                keys["valid", i] = send(
                    valid_send.at[i - 1], valid_recv.at[i], at_x(lax.rem(x + i, nx))
                )

    def send_counts():
        counts = counts_of()
        filled = valid_recv[0]
        for i in range(1, nx):
            arrived(keys["valid", i], valid_recv.at[i])
            filled = filled + valid_recv[i]
        empty = (float(NQ * quarter_rows) - filled) * float(h_local)
        count_recv[g] = counts - jnp.where(iota((8, NB), 1) == 0, empty, 0.0)
        for q in range(1, ng):
            keys["count", q] = send(count_recv.at[g], count_recv.at[g], at_g(lax.rem(g + q, ng)))

    def send_threshold():
        for q in range(1, ng):
            arrived(keys["count", q], count_recv.at[lax.rem(g + ng - q, ng)])
        counts = count_recv[0]
        for q in range(1, ng):
            counts = counts + count_recv[q]
        sums = jnp.sum(counts, axis=1, keepdims=True)
        below = mask_f32(iota((NB, NB), 0) < iota((NB, NB), 1))
        before_bin = dot(counts, below, HIGHEST)
        fraction = jnp.clip((QUANTILE * sums - before_bin) / jnp.maximum(counts, 1.0), 0.0, 1.0)
        threshold = (HIST_TOP / NB) * jnp.sum(fraction, axis=1, keepdims=True)
        th_send[...] = jnp.broadcast_to(threshold, (8, 128))
        th_recv[0] = th_send[...]
        for j in range(1, nz):
            keys["th", j] = send(th_send, th_recv.at[j], at_z(plane(j)))

    def share_thresholds():
        gathered = jnp.zeros((8, 128), F32)
        for j in range(nz):
            if j:
                arrived(keys["th", j], th_recv.at[j])
            place = x * nz + plane(-j)
            gathered = jnp.where(iota((8, 128), 1) == place, th_recv[j], gathered)
        tx_send[...] = gathered
        for i in range(1, nx):
            keys["tx", i] = send(tx_send, tx_recv.at[i - 1], at_x(lax.rem(x + i, nx)))

    plan = [(FIRST - 1.0, lambda _: send_valid(), 0)]
    for n in range(NQ):
        for after, step in zip(
            AFTER, (select, rows_1, rows_2, rows_3, rows_4, hid_2, hid_3, z_return), strict=True
        ):
            plan.append((FIRST + SPACING * n + after, step, n))
    split_weights()
    home_weights()
    for _, step, n in sorted(plan, key=lambda entry: entry[0]):
        step(n)

    combine(0)
    combine(1)
    share_thresholds()
    combine(2)
    gathered = tx_send[...]
    for i in range(1, nx):
        arrived(keys["tx", i], tx_recv.at[i - 1])
        gathered = gathered + tx_recv[i - 1]
    thresholds[...] = gathered[0:1, : nx * nz]
    for copy in started:
        copy.wait_send()
    combine(3)


def per_device(nx, nz, tokens, routes, route_weights, slots, gate_up, down):
    ng = NY * NC
    t_count, width = tokens.shape
    picks = routes.shape[1]
    feat = width // ng
    half_f = feat // 2
    h_local = down.shape[1]
    part_rows = nz // NQ * CAP
    quarter_rows = nx * part_rows
    back_rows = 2 * nx * CAP
    size = 2 * quarter_rows
    wide = 16 if quarter_rows % 32 == 0 else 2

    vmem = pl.BlockSpec(memory_space=pltpu.VMEM)
    hbm = pl.BlockSpec(memory_space=pl.ANY)
    mixed, thresholds = pl.pallas_call(
        functools.partial(kernel, nx, nz),
        out_shape=(
            jax.ShapeDtypeStruct((t_count, feat), BF16),
            jax.ShapeDtypeStruct((1, slots.shape[0]), F32),
        ),
        in_specs=[hbm] * 6,
        out_specs=(vmem, vmem),
        scratch_shapes=[
            pltpu.SMEM(slots.shape, jnp.int32),
            pltpu.VMEM((picks, t_count), jnp.int32),
            pltpu.VMEM((picks, t_count), F32),
            pltpu.VMEM((t_count, feat), BF16),
            pltpu.VMEM((nz, back_rows, half_f), BF16),
            pltpu.VMEM((nz, back_rows, half_f), BF16),
            pltpu.VMEM((NQ, nx - 1, 2 * part_rows, half_f), BF16),
            pltpu.VMEM((ng, NQ, nx, 2 * part_rows, half_f), BF16),
            pltpu.VMEM((2 * width, h_local), BF16),
            pltpu.VMEM((ng, half_f, 4 * h_local), BF16),
            pltpu.VMEM((ng, h_local, feat), BF16),
            pltpu.VMEM((NQ, size, 4 * h_local), F32),
            pltpu.VMEM((ng, NQ, quarter_rows, h_local), BF16),
            pltpu.VMEM((NQ, nx - 1, 2 * part_rows, half_f), BF16),
            pltpu.VMEM((NQ, nx, 2 * part_rows, half_f), BF16),
            pltpu.VMEM((nz, back_rows, half_f), BF16),
            pltpu.VMEM((nz, back_rows, half_f), BF16),
            pltpu.VMEM((size, size), BF16),
            pltpu.VMEM((size, size), BF16),
            pltpu.VMEM((NQ, t_count, size), BF16),
            pltpu.VMEM((NQ, t_count, size), BF16),
            pltpu.VMEM((t_count, feat), F32),
            pltpu.VMEM((8 * wide, 32 * wide), F32),
            pltpu.VMEM((nz, 8, 128), F32),
            pltpu.VMEM((nz, 8, 128), F32),
            pltpu.VMEM((nx - 1, 8, 128), F32),
            pltpu.VMEM((nx, 8, 128), F32),
            pltpu.VMEM((ng, 8, 128), F32),
            pltpu.VMEM((8, 128), F32),
            pltpu.VMEM((nz, 8, 128), F32),
            pltpu.VMEM((8, 128), F32),
            pltpu.VMEM((nx - 1, 8, 128), F32),
            pltpu.SemaphoreType.DMA((SEMS,)),
            pltpu.SemaphoreType.DMA((SEMS,)),
            pltpu.SemaphoreType.DMA((6,)),
        ],
        compiler_params=pltpu.CompilerParams(
            collective_id=0, has_side_effects=True, vmem_limit_bytes=60 << 20
        ),
        cost_estimate=pl.CostEstimate(
            flops=4 << 30, bytes_accessed=8 << 20, transcendentals=1 << 17
        ),
    )(
        tokens,
        routes.T,
        route_weights.T,
        slots,
        gate_up.reshape(2 * width, h_local),
        down[0],
    )
    return mixed, thresholds.reshape(-1)


def solution(mesh, nx=NX, nz=NZ):
    placed = (
        P("ep", None),
        P("ep", None),
        P("ep", None),
        P(),
        P("ep", None, None, "grp"),
        P("ep", "grp", None),
    )
    return jax.shard_map(
        functools.partial(per_device, nx, nz),
        mesh=mesh,
        in_specs=placed,
        out_specs=(P("ep", "grp"), P()),
        check_vma=False,
    )
```

```python
import functools

import jax
import jax.numpy as jnp
from jax import lax
from jax.experimental import pallas as pl
from jax.experimental.pallas import tpu as pltpu
from jax.sharding import PartitionSpec as P

NB = 128
CAP = 10
NY = 4
NC = 2
NX = 4
NZ = 16
NQ = 4
HIST_TOP = 16.0
QUANTILE = 0.999
MESH = pl.DeviceIdType.MESH
F32 = jnp.float32
BF16 = jnp.bfloat16
HIGHEST = lax.Precision.HIGHEST
SEMS = 220
ORDER = (
    0, 1, 10, 11, 2, 20, 21, 12, 30, 40, 50, 3,
    31, 22, 41, 60, 13, 70, 51, 32, 61, 42, 71, 80,
    23, 52, 62, 81, 72, 33, 43, 53, 82, 63, 73, 83,
)


def dot(a, b, precision=None):
    return jnp.dot(a, b, preferred_element_type=F32, precision=precision)


def dot_nt(a, b, precision=None):
    return lax.dot_general(
        a, b, (((1,), (1,)), ((), ())), preferred_element_type=F32, precision=precision
    )


def mask_f32(m):
    return jnp.where(m, 1.0, 0.0)


def mask_bf16(m):
    return mask_f32(m).astype(BF16)


def iota(shape, dim):
    return lax.broadcasted_iota(jnp.int32, shape, dim)


def split(value, by):
    whole = jnp.floor((value + 0.5) * (1.0 / by))
    return whole, value - whole * by


def kernel(
    nx,
    nz,
    tokens,
    routes_t,
    weights_t,
    slots_hbm,
    gate_up,
    down,
    mixed,
    thresholds,
    slots,
    routes_v,
    weights_v,
    own_tokens,
    fwd_send,
    fwd,
    xsend,
    rows,
    w_raw,
    w_split,
    dn,
    acc,
    hid,
    outs,
    outr,
    zsend,
    zrecv,
    perm_in,
    perm_out,
    weights_hi,
    weights_lo,
    total,
    hist,
    plane_send,
    plane_recv,
    valid_send,
    valid_recv,
    count_recv,
    th_send,
    th_recv,
    tx_send,
    tx_recv,
    send_sems,
    recv_sems,
    local_sems,
):
    ng = NY * NC
    planes = nz // NQ
    part_rows = planes * CAP
    quarter_rows = nx * part_rows
    t_count = tokens.shape[0]
    feat = tokens.shape[1] // ng
    half_f = feat // 2
    h_local = down.shape[0]
    picks = routes_t.shape[0]
    back_rows = 2 * nx * CAP

    g = lax.axis_index("grp")
    ep = lax.axis_index("ep")
    y, c = lax.div(g, NC), lax.rem(g, NC)
    x, z = lax.div(ep, nz), lax.rem(ep, nz)
    other = 1 - c

    def g_of(yy, cc):
        return yy * NC + cc

    g_up = g_of(lax.rem(y + 1, NY), c)
    g_dn = g_of(lax.rem(y + NY - 1, NY), c)
    g_op = g_of(lax.rem(y + 2, NY), c)
    g_mate = g_of(y, other)

    def mate_of(q):
        return q + other - c

    offsets = [8, 0, 2, -2, 1, -1, 5, -5, 3, -3, 7, -7, 4, -4, 6, -6] if nz == 16 else [1, -1, 2, 0]

    def offset(s):
        return offsets[s]

    def plane(j):
        return lax.rem(z + j + nz, nz)

    def at_z(zz):
        return (g, x * nz + zz)

    def at_x(xx):
        return (g, xx * nz + z)

    def at_g(gg):
        return (gg, ep)

    started = []
    used = [0]

    def send(src, dst, device):
        k = used[0]
        used[0] += 1
        copy = pltpu.make_async_remote_copy(
            src_ref=src,
            dst_ref=dst,
            send_sem=send_sems.at[k],
            recv_sem=recv_sems.at[k],
            device_id=device,
            device_id_type=MESH,
        )
        copy.start()
        started.append(copy)
        return k

    def arrived(k, ref):
        pltpu.make_async_remote_copy(
            src_ref=ref,
            dst_ref=ref,
            send_sem=send_sems.at[k],
            recv_sem=recv_sems.at[k],
            device_id=(g, ep),
            device_id_type=MESH,
        ).wait_recv()

    def take(src, dst, k):
        copy = pltpu.make_async_copy(src, dst, local_sems.at[k])
        copy.start()
        return copy

    mine = pl.ds(pl.multiple_of(g * feat, 128), feat)
    take_routes = take(routes_t, routes_v, 0)
    take_tokens = take(tokens.at[:, mine], own_tokens, 1)
    take_slots = take(slots_hbm, slots, 2)
    take_weights = take(weights_t, weights_v, 3)
    take_w = take(gate_up, w_raw, 4)
    take_down = take(down.at[:, mine], dn.at[g], 5)

    barrier = pltpu.get_barrier_semaphore()
    peers = (
        [at_z(lax.rem(z + j, nz)) for j in range(1, nz)]
        + [at_x(lax.rem(x + i, nx)) for i in range(1, nx)]
        + [at_g(lax.rem(g + q, ng)) for q in range(1, ng)]
    )
    for peer in peers:
        pl.semaphore_signal(barrier, inc=1, device_id=peer, device_id_type=MESH)

    take_routes.wait()
    take_slots.wait()
    routes_f = routes_v[...].astype(F32)
    lines = nz * nx
    experts = jnp.full((lines, 1), -1.0, F32)
    for s in range(nz):
        for i in range(nx):
            e = slots[lax.rem(x + i, nx) * nz + plane(offset(s))].astype(F32)
            experts = jnp.where(iota((lines, 1), 0) == s * nx + i, e, experts)
    chosen = jnp.zeros((lines, t_count), F32)
    for k in range(picks):
        chosen = jnp.where(routes_f[k : k + 1, :] == experts, 1.0, chosen)
    tri = mask_bf16(iota((t_count, t_count), 0) < iota((t_count, t_count), 1))
    earlier = dot(chosen.astype(BF16), tri)
    code = jnp.where(chosen > 0.5, earlier, -100.0)
    number = jnp.sum(chosen, axis=1, keepdims=True)
    def pack(value):
        return jnp.concatenate([value[:, :half_f], value[:, half_f:]], axis=0).astype(BF16)

    take_tokens.wait()
    row = iota((nx * CAP, t_count), 0).astype(F32)
    keys = {}

    def dispatch(n):
        sel = []
        for s in range(n * planes, (n + 1) * planes):
            wanted = jnp.zeros((nx * CAP, t_count), F32)
            for i in range(nx):
                place = code[s * nx + i : s * nx + i + 1, :] + float(i * CAP)
                wanted = jnp.where(row == place, 1.0, wanted)
            sel.append(wanted)
        picked = dot(jnp.concatenate(sel, axis=0).astype(BF16), own_tokens[...])
        for k in range(planes):
            s = n * planes + k
            packed = pack(picked[k * nx * CAP : (k + 1) * nx * CAP])
            if offset(s) == 0:
                fwd[s] = packed
            else:
                fwd_send[s] = packed

    def dispatch_send(n):
        for s in range(n * planes, (n + 1) * planes):
            if offset(s):
                to = at_z(plane(offset(s)))
                keys["fwd", s] = send(fwd_send.at[s], fwd.at[s], to)

    dispatch(0)
    pl.semaphore_wait(barrier, len(peers))
    down_keys = []
    for q in range(1, ng):
        to = lax.rem(g + q, ng)
        columns = pl.ds(pl.multiple_of(to * feat, 128), feat)
        down_keys.append(send(down.at[:, columns], dn.at[g], at_g(to)))
    dispatch_send(0)
    for n in range(1, NQ):
        dispatch(n)
        dispatch_send(n)

    for s in range(nz):
        for i in range(nx):
            line = jnp.broadcast_to(number[s * nx + i : s * nx + i + 1, :], (1, 128))
            plane_send[s, i : i + 1, :] = line
        plane_send[s, nx:8, :] = jnp.zeros((8 - nx, 128), F32)
    for s in range(nz):
        if offset(s) == 0:
            plane_recv[s] = plane_send[s]
        else:
            keys["plane", s] = send(plane_send.at[s], plane_recv.at[s], at_z(plane(offset(s))))
    hist[...] = jnp.zeros_like(hist)

    def swap(a, b):
        row = iota((2 * quarter_rows, 1), 0).astype(F32)
        j, row = split(row, 2 * a * CAP)
        half, row = split(row, a * CAP)
        i, p = split(row, CAP)
        source = i * (2.0 * b * CAP) + half * (b * CAP) + j * CAP + p
        return mask_bf16(iota((2 * quarter_rows, 2 * quarter_rows), 1).astype(F32) == source)

    size = 2 * quarter_rows
    perm_in[...] = swap(planes, nx)
    perm_out[...] = swap(nx, planes)

    def split_weights():
        take_w.wait()
        wide = 2 * 128
        r, q = iota((wide, wide), 0), iota((wide, wide), 1)
        order = mask_bf16(q == jnp.where(r < 128, 2 * r, 2 * (r - 128) + 1))
        per = feat // 128

        @pl.loop(0, ng)
        def _(gg):
            for b in range(per):
                first = pl.multiple_of((gg * per + b) * wide, wide)
                parted = dot(order, w_raw[pl.ds(first, wide)]).astype(BF16)
                half, b = b * 128 // half_f, b * 128 % half_f
                to = 2 * h_local * half
                w_split[gg, b : b + 128, to : to + h_local] = parted[:128]
                w_split[gg, b : b + 128, to + h_local : to + 2 * h_local] = parted[128:]

    def home_weights():
        take_weights.wait()
        eye = mask_f32(iota((t_count, t_count), 0) == iota((t_count, t_count), 1))
        routes_c = dot_nt(eye, routes_v[...].astype(F32), HIGHEST)
        weights_c = dot_nt(eye, weights_v[...], HIGHEST)
        before = mask_bf16(iota((t_count, t_count), 1) < iota((t_count, t_count), 0))
        lane_k, in_plane = split(iota((1, size), 1).astype(F32), back_rows)
        _, entry = split(in_plane, nx * CAP)
        lane_i, place = split(entry, CAP)
        for quarter in range(NQ):
            expert = jnp.full((1, size), -1.0, F32)
            for k in range(planes):
                j = offset(quarter * planes + k)
                for i in range(nx):
                    e = slots[lax.rem(x + i, nx) * nz + plane(j)].astype(F32)
                    expert = jnp.where((lane_k == k) & (lane_i == i), e, expert)
            hit = jnp.zeros((t_count, size), F32)
            weight = hit
            for k in range(picks):
                eq = routes_c[:, k : k + 1] == expert
                hit = jnp.where(eq, 1.0, hit)
                weight = jnp.where(eq, weights_c[:, k : k + 1], weight)
            earlier = dot(before, hit.astype(BF16))
            weight = jnp.where((hit > 0.5) & (earlier == place), weight, 0.0)
            top = weight.astype(BF16)
            weights_hi[quarter] = top
            weights_lo[quarter] = (weight - top.astype(F32)).astype(BF16)

    def select(n):
        for s in range(n * planes, (n + 1) * planes):
            if offset(s):
                arrived(keys["fwd", s], fwd.at[s])
        block = fwd[n * planes : (n + 1) * planes].reshape(size, half_f)
        moved = dot(perm_in[...], block).astype(BF16)
        for i in range(nx):
            part = moved[i * 2 * part_rows : (i + 1) * 2 * part_rows]
            if i == 0:
                rows[g, n, 0] = part
            else:
                xsend[n, i - 1] = part
                keys["x", n, i] = send(
                    xsend.at[n, i - 1], rows.at[g, n, i], at_x(lax.rem(x + i, nx))
                )

    def rows_1(n):
        for i in range(1, nx):
            arrived(keys["x", n, i], rows.at[g, n, i])
        own = rows.at[g, n]
        keys["r_up", n] = send(own, own, at_g(g_up))
        keys["r_dn", n] = send(own, own, at_g(g_dn))
        keys["r_mate", n] = send(own, own, at_g(g_mate))

    near, far = pl.ds(0, nx // 2), pl.ds(nx // 2, nx // 2)

    def rows_2(n):
        ref = rows.at[g_dn, n]
        arrived(keys["r_up", n], ref)
        keys["r_up2", n] = send(rows.at[g_dn, n, near], rows.at[g_dn, n, near], at_g(g_up))
        keys["m_dn", n] = send(ref, ref, at_g(g_mate))
        ref = rows.at[g_up, n]
        arrived(keys["r_dn", n], ref)
        keys["r_dn2", n] = send(rows.at[g_up, n, far], rows.at[g_up, n, far], at_g(g_dn))
        keys["m_up", n] = send(ref, ref, at_g(g_mate))

    def rows_3(n):
        ref = rows.at[g_op, n, near]
        arrived(keys["r_up2", n], ref)
        keys["m_op1", n] = send(ref, ref, at_g(g_mate))
        ref = rows.at[g_op, n, far]
        arrived(keys["r_dn2", n], ref)
        keys["m_op2", n] = send(ref, ref, at_g(g_mate))
        gate_and_up(n, c)

    def rows_4(n):
        arrived(keys["r_mate", n], rows.at[g_mate, n])
        arrived(keys["m_dn", n], rows.at[mate_of(g_dn), n])
        arrived(keys["m_up", n], rows.at[mate_of(g_up), n])
        arrived(keys["m_op1", n], rows.at[mate_of(g_op), n, near])
        arrived(keys["m_op2", n], rows.at[mate_of(g_op), n, far])
        gate_and_up(n, other)
        activate(n)
        own = hid.at[g, n]
        for name, to in (("up", g_up), ("dn", g_dn), ("op", g_op), ("mate", g_mate)):
            keys["h_" + name, n] = send(own, own, at_g(to))

    def hid_2(n):
        for name, src in (("up", g_dn), ("dn", g_up), ("op", g_op)):
            ref = hid.at[src, n]
            arrived(keys["h_" + name, n], ref)
            keys["hm_" + name, n] = send(ref, ref, at_g(g_mate))

    def hid_3(n):
        if n == 0:
            take_down.wait()
            for q in range(1, ng):
                arrived(down_keys[q - 1], dn.at[lax.rem(g + ng - q, ng)])
        arrived(keys["h_mate", n], hid.at[g_mate, n])
        for name, src in (("up", g_dn), ("dn", g_up), ("op", g_op)):
            arrived(keys["hm_" + name, n], hid.at[mate_of(src), n])
        output_rows(n)
        if n == NQ - 1:
            send_threshold()

    def gate_and_up(n, core):
        if n not in begun:
            begun.append(n)
            acc[n] = jnp.zeros((size, 4 * h_local), F32)

        @pl.loop(0, NY)
        def _(yy):
            q = g_of(yy, core)
            acc[n] += dot(rows[q, n].reshape(size, half_f), w_split[q])

    begun = []

    def activate(n):
        both = []
        for i in range(nx):
            r = 2 * part_rows * i
            both.append(
                acc[n, r : r + part_rows, : 2 * h_local]
                + acc[n, r + part_rows : r + 2 * part_rows, 2 * h_local :]
            )
        both = jnp.concatenate(both, axis=0)
        gate = both[:, :h_local]
        hid[g, n] = (gate / (1.0 + jnp.exp(-gate)) * both[:, h_local:]).astype(BF16)

    wide = hist.shape[0] // 8

    def histogram(n):
        @pl.loop(0, quarter_rows // (2 * wide))
        def _(step):
            first = pl.multiple_of(step * 2 * wide, 2 * wide)
            level = jnp.abs(hid[g, n, pl.ds(first, 2 * wide)].astype(F32))
            where = jnp.clip(level * (NB / HIST_TOP) - 0.5, 0.0, NB - 1.0)
            lower = jnp.floor(where)
            part = where - lower
            coarse = jnp.floor(lower * (1.0 / 16.0))
            fine = lower - 16.0 * coarse
            eight = iota((8, h_local), 0).astype(F32)
            sixteen = iota((16, h_local), 0).astype(F32)
            sides = []
            for side in range(2):
                left, one, share = [], [], []
                for r in range(side * wide, (side + 1) * wide):
                    left.append(mask_f32(coarse[r : r + 1] == eight))
                    match = fine[r : r + 1] == sixteen
                    one.append(mask_f32(match))
                    share.append(jnp.where(match, part[r : r + 1], 0.0))
                sides.append(
                    (
                        jnp.concatenate(left, axis=0).astype(BF16),
                        jnp.concatenate(one + share, axis=0).astype(BF16),
                    )
                )
            a = jnp.concatenate([sides[0][0], sides[1][0]], axis=1)
            b = jnp.concatenate([sides[0][1], sides[1][1]], axis=1)
            hist[...] += dot_nt(a, b)

    def counts_of():
        m, k = 8 * wide, 16 * wide
        own_row = lax.shift_right_logical(iota((m, k), 0), 3) == lax.shift_right_logical(
            iota((m, k), 1), 4
        )
        fold = mask_f32((iota((k, NB), 0) & 15) == (iota((k, NB), 1) & 15))
        own_bin = (iota((m, NB), 0) & 7) == lax.shift_right_logical(iota((m, NB), 1), 4)

        def bins(table):
            folded = dot(jnp.where(own_row, table, 0.0), fold, HIGHEST)
            return jnp.sum(jnp.where(own_bin, folded, 0.0), axis=0, keepdims=True)

        number = bins(hist[:, :k])
        share = jnp.broadcast_to(bins(hist[:, k:]), (8, NB))
        return jnp.broadcast_to(number, (8, NB)) - share + pltpu.roll(share, 1, 1)

    def output_rows(n):
        full = jnp.concatenate([hid[q, n] for q in range(ng)], axis=1)
        made = dot(full, dn[...].reshape(ng * h_local, feat))
        for i in range(nx):
            packed = pack(made[i * part_rows : (i + 1) * part_rows])
            if i == 0:
                outr[n, 0] = packed
            else:
                outs[n, i - 1] = packed
                keys["out", n, i] = send(
                    outs.at[n, i - 1], outr.at[n, i], at_x(lax.rem(x + nx - i, nx))
                )

    def z_return(n):
        for i in range(1, nx):
            arrived(keys["out", n, i], outr.at[n, i])
        moved = dot(perm_out[...], outr[n].reshape(size, half_f)).astype(BF16)
        for k in range(planes):
            s = n * planes + k
            block = moved[k * back_rows : (k + 1) * back_rows]
            j = offset(s)
            if j == 0:
                zrecv[s] = block
            else:
                zsend[s] = block
                keys["back", s] = send(zsend.at[s], zrecv.at[s], at_z(plane(-j)))

    def combine(n):
        for s in range(n * planes, (n + 1) * planes):
            if offset(s):
                arrived(keys["back", s], zrecv.at[s])
        back = zrecv[n * planes : (n + 1) * planes].reshape(size, half_f)
        _, in_plane = split(iota((1, size), 1).astype(F32), back_rows)
        upper = in_plane < nx * CAP
        zero = jnp.zeros((), BF16)
        for half in range(2):
            keep = upper if half == 0 else jnp.logical_not(upper)
            high = jnp.where(keep, weights_hi[n], zero)
            low = jnp.where(keep, weights_lo[n], zero)
            gained = dot(high, back) + dot(low, back)
            cols = slice(half * half_f, (half + 1) * half_f)
            if n > 0:
                gained = total[:, cols] + gained
            if n < NQ - 1:
                total[:, cols] = gained
            else:
                mixed[:, cols] = gained.astype(BF16)

    def send_valid():
        number = jnp.zeros((8, 128), F32)
        for s in range(nz):
            if offset(s):
                arrived(keys["plane", s], plane_recv.at[s])
            number = number + plane_recv[s]
        for i in range(nx):
            line = jnp.broadcast_to(number[i : i + 1, :], (8, 128))
            if i == 0:
                valid_recv[0] = line
            else:
                valid_send[i - 1] = line
                keys["valid", i] = send(
                    valid_send.at[i - 1], valid_recv.at[i], at_x(lax.rem(x + i, nx))
                )

    def send_counts():
        counts = counts_of()
        filled = valid_recv[0]
        for i in range(1, nx):
            arrived(keys["valid", i], valid_recv.at[i])
            filled = filled + valid_recv[i]
        empty = (float(NQ * quarter_rows) - filled) * float(h_local)
        count_recv[g] = counts - jnp.where(iota((8, NB), 1) == 0, empty, 0.0)
        for q in range(1, ng):
            keys["count", q] = send(count_recv.at[g], count_recv.at[g], at_g(lax.rem(g + q, ng)))

    def send_threshold():
        for q in range(1, ng):
            arrived(keys["count", q], count_recv.at[lax.rem(g + ng - q, ng)])
        counts = count_recv[0]
        for q in range(1, ng):
            counts = counts + count_recv[q]
        sums = jnp.sum(counts, axis=1, keepdims=True)
        below = mask_f32(iota((NB, NB), 0) < iota((NB, NB), 1))
        before_bin = dot(counts, below, HIGHEST)
        fraction = jnp.clip((QUANTILE * sums - before_bin) / jnp.maximum(counts, 1.0), 0.0, 1.0)
        threshold = (HIST_TOP / NB) * jnp.sum(fraction, axis=1, keepdims=True)
        th_send[...] = jnp.broadcast_to(threshold, (8, 128))
        th_recv[0] = th_send[...]
        for j in range(1, nz):
            keys["th", j] = send(th_send, th_recv.at[j], at_z(plane(j)))

    def share_thresholds():
        gathered = jnp.zeros((8, 128), F32)
        for j in range(nz):
            if j:
                arrived(keys["th", j], th_recv.at[j])
            place = x * nz + plane(-j)
            gathered = jnp.where(iota((8, 128), 1) == place, th_recv[j], gathered)
        tx_send[...] = gathered
        for i in range(1, nx):
            keys["tx", i] = send(tx_send, tx_recv.at[i - 1], at_x(lax.rem(x + i, nx)))

    steps = (select, rows_1, rows_2, rows_3, rows_4, histogram, hid_2, hid_3, z_return)
    split_weights()
    home_weights()
    for entry in ORDER:
        if entry == 51:
            send_valid()
        steps[entry // 10](entry % 10)
        if entry == 53:
            send_counts()

    combine(0)
    combine(1)
    share_thresholds()
    combine(2)
    gathered = tx_send[...]
    for i in range(1, nx):
        arrived(keys["tx", i], tx_recv.at[i - 1])
        gathered = gathered + tx_recv[i - 1]
    thresholds[...] = gathered[0:1, : nx * nz]
    for copy in started:
        copy.wait_send()
    combine(3)


def per_device(nx, nz, tokens, routes, route_weights, slots, gate_up, down):
    ng = NY * NC
    t_count, width = tokens.shape
    picks = routes.shape[1]
    feat = width // ng
    half_f = feat // 2
    h_local = down.shape[1]
    part_rows = nz // NQ * CAP
    quarter_rows = nx * part_rows
    back_rows = 2 * nx * CAP
    size = 2 * quarter_rows
    wide = 16 if quarter_rows % 32 == 0 else 2

    vmem = pl.BlockSpec(memory_space=pltpu.VMEM)
    hbm = pl.BlockSpec(memory_space=pl.ANY)
    mixed, thresholds = pl.pallas_call(
        functools.partial(kernel, nx, nz),
        out_shape=(
            jax.ShapeDtypeStruct((t_count, feat), BF16),
            jax.ShapeDtypeStruct((1, slots.shape[0]), F32),
        ),
        in_specs=[hbm] * 6,
        out_specs=(vmem, vmem),
        scratch_shapes=[
            pltpu.SMEM(slots.shape, jnp.int32),
            pltpu.VMEM((picks, t_count), jnp.int32),
            pltpu.VMEM((picks, t_count), F32),
            pltpu.VMEM((t_count, feat), BF16),
            pltpu.VMEM((nz, back_rows, half_f), BF16),
            pltpu.VMEM((nz, back_rows, half_f), BF16),
            pltpu.VMEM((NQ, nx - 1, 2 * part_rows, half_f), BF16),
            pltpu.VMEM((ng, NQ, nx, 2 * part_rows, half_f), BF16),
            pltpu.VMEM((2 * width, h_local), BF16),
            pltpu.VMEM((ng, half_f, 4 * h_local), BF16),
            pltpu.VMEM((ng, h_local, feat), BF16),
            pltpu.VMEM((NQ, size, 4 * h_local), F32),
            pltpu.VMEM((ng, NQ, quarter_rows, h_local), BF16),
            pltpu.VMEM((NQ, nx - 1, 2 * part_rows, half_f), BF16),
            pltpu.VMEM((NQ, nx, 2 * part_rows, half_f), BF16),
            pltpu.VMEM((nz, back_rows, half_f), BF16),
            pltpu.VMEM((nz, back_rows, half_f), BF16),
            pltpu.VMEM((size, size), BF16),
            pltpu.VMEM((size, size), BF16),
            pltpu.VMEM((NQ, t_count, size), BF16),
            pltpu.VMEM((NQ, t_count, size), BF16),
            pltpu.VMEM((t_count, feat), F32),
            pltpu.VMEM((8 * wide, 32 * wide), F32),
            pltpu.VMEM((nz, 8, 128), F32),
            pltpu.VMEM((nz, 8, 128), F32),
            pltpu.VMEM((nx - 1, 8, 128), F32),
            pltpu.VMEM((nx, 8, 128), F32),
            pltpu.VMEM((ng, 8, 128), F32),
            pltpu.VMEM((8, 128), F32),
            pltpu.VMEM((nz, 8, 128), F32),
            pltpu.VMEM((8, 128), F32),
            pltpu.VMEM((nx - 1, 8, 128), F32),
            pltpu.SemaphoreType.DMA((SEMS,)),
            pltpu.SemaphoreType.DMA((SEMS,)),
            pltpu.SemaphoreType.DMA((6,)),
        ],
        compiler_params=pltpu.CompilerParams(
            collective_id=0, has_side_effects=True, vmem_limit_bytes=60 << 20
        ),
        cost_estimate=pl.CostEstimate(
            flops=4 << 30, bytes_accessed=8 << 20, transcendentals=1 << 17
        ),
    )(
        tokens,
        routes.T,
        route_weights.T,
        slots,
        gate_up.reshape(2 * width, h_local),
        down[0],
    )
    return mixed, thresholds.reshape(-1)


def solution(mesh, nx=NX, nz=NZ):
    placed = (
        P("ep", None),
        P("ep", None),
        P("ep", None),
        P(),
        P("ep", None, None, "grp"),
        P("ep", "grp", None),
    )
    return jax.shard_map(
        functools.partial(per_device, nx, nz),
        mesh=mesh,
        in_specs=placed,
        out_specs=(P("ep", "grp"), P()),
        check_vma=False,
    )
```

```python
import functools

import jax
import jax.numpy as jnp
from jax import lax
from jax.experimental import pallas as pl
from jax.experimental.pallas import tpu as pltpu
from jax.sharding import PartitionSpec as P

NB = 128
CAP = 10
NY = 4
NC = 2
NX = 4
NZ = 16
NQ = 4
HIST_TOP = 16.0
QUANTILE = 0.999
MESH = pl.DeviceIdType.MESH
F32 = jnp.float32
BF16 = jnp.bfloat16
HIGHEST = lax.Precision.HIGHEST
SEMS = 220
ORDER = (
    0, 1, 10, 11, 2, 20, 21, 12, 30, 40, 50, 3,
    31, 22, 41, 60, 13, 70, 51, 32, 61, 42, 71, 80,
    23, 52, 62, 81, 72, 33, 43, 53, 82, 63, 73, 83,
)


def dot(a, b, precision=None):
    return jnp.dot(a, b, preferred_element_type=F32, precision=precision)


def dot_nt(a, b, precision=None):
    return lax.dot_general(
        a, b, (((1,), (1,)), ((), ())), preferred_element_type=F32, precision=precision
    )


def mask_f32(m):
    return jnp.where(m, 1.0, 0.0)


def mask_bf16(m):
    return mask_f32(m).astype(BF16)


def iota(shape, dim):
    return lax.broadcasted_iota(jnp.int32, shape, dim)


def split(value, by):
    whole = jnp.floor((value + 0.5) * (1.0 / by))
    return whole, value - whole * by


def kernel(
    nx,
    nz,
    tokens,
    routes_t,
    weights_t,
    slots_hbm,
    gate_up,
    down,
    mixed,
    thresholds,
    slots,
    routes_v,
    weights_v,
    own_tokens,
    fwd_send,
    fwd,
    xsend,
    rows,
    w_raw,
    w_split,
    dn,
    acc,
    hid,
    outs,
    outr,
    zsend,
    zrecv,
    perm_in,
    perm_out,
    weights_hi,
    weights_lo,
    total,
    hist,
    plane_send,
    plane_recv,
    valid_send,
    valid_recv,
    count_recv,
    th_send,
    th_recv,
    tx_send,
    tx_recv,
    send_sems,
    recv_sems,
    local_sems,
):
    ng = NY * NC
    planes = nz // NQ
    part_rows = planes * CAP
    quarter_rows = nx * part_rows
    t_count = tokens.shape[0]
    feat = tokens.shape[1] // ng
    half_f = feat // 2
    h_local = down.shape[0]
    picks = routes_t.shape[0]
    back_rows = 2 * nx * CAP

    g = lax.axis_index("grp")
    ep = lax.axis_index("ep")
    y, c = lax.div(g, NC), lax.rem(g, NC)
    x, z = lax.div(ep, nz), lax.rem(ep, nz)
    other = 1 - c

    def g_of(yy, cc):
        return yy * NC + cc

    g_up = g_of(lax.rem(y + 1, NY), c)
    g_dn = g_of(lax.rem(y + NY - 1, NY), c)
    g_op = g_of(lax.rem(y + 2, NY), c)
    g_mate = g_of(y, other)

    def mate_of(q):
        return q + other - c

    offsets = [8, 0, 2, -2, 1, -1, 5, -5, 3, -3, 7, -7, 4, -4, 6, -6] if nz == 16 else [1, -1, 2, 0]

    def offset(s):
        return offsets[s]

    def plane(j):
        return lax.rem(z + j + nz, nz)

    def at_z(zz):
        return (g, x * nz + zz)

    def at_x(xx):
        return (g, xx * nz + z)

    def at_g(gg):
        return (gg, ep)

    started = []
    used = [0]

    def send(src, dst, device):
        k = used[0]
        used[0] += 1
        copy = pltpu.make_async_remote_copy(
            src_ref=src,
            dst_ref=dst,
            send_sem=send_sems.at[k],
            recv_sem=recv_sems.at[k],
            device_id=device,
            device_id_type=MESH,
        )
        copy.start()
        started.append(copy)
        return k

    def arrived(k, ref):
        pltpu.make_async_remote_copy(
            src_ref=ref,
            dst_ref=ref,
            send_sem=send_sems.at[k],
            recv_sem=recv_sems.at[k],
            device_id=(g, ep),
            device_id_type=MESH,
        ).wait_recv()

    def take(src, dst, k):
        copy = pltpu.make_async_copy(src, dst, local_sems.at[k])
        copy.start()
        return copy

    mine = pl.ds(pl.multiple_of(g * feat, 128), feat)
    take_routes = take(routes_t, routes_v, 0)
    take_tokens = take(tokens.at[:, mine], own_tokens, 1)
    take_slots = take(slots_hbm, slots, 2)
    take_weights = take(weights_t, weights_v, 3)
    take_w = take(gate_up, w_raw, 4)
    take_down = take(down.at[:, mine], dn.at[g], 5)

    barrier = pltpu.get_barrier_semaphore()
    peers = (
        [at_z(lax.rem(z + j, nz)) for j in range(1, nz)]
        + [at_x(lax.rem(x + i, nx)) for i in range(1, nx)]
        + [at_g(lax.rem(g + q, ng)) for q in range(1, ng)]
    )
    for peer in peers:
        pl.semaphore_signal(barrier, inc=1, device_id=peer, device_id_type=MESH)

    take_routes.wait()
    take_slots.wait()
    routes_f = routes_v[...].astype(F32)
    lines = nz * nx
    experts = jnp.full((lines, 1), -1.0, F32)
    for s in range(nz):
        for i in range(nx):
            e = slots[lax.rem(x + i, nx) * nz + plane(offset(s))].astype(F32)
            experts = jnp.where(iota((lines, 1), 0) == s * nx + i, e, experts)
    chosen = jnp.zeros((lines, t_count), F32)
    for k in range(picks):
        chosen = jnp.where(routes_f[k : k + 1, :] == experts, 1.0, chosen)
    tri = mask_bf16(iota((t_count, t_count), 0) < iota((t_count, t_count), 1))
    earlier = dot(chosen.astype(BF16), tri)
    code = jnp.where(chosen > 0.5, earlier, -100.0)
    number = jnp.sum(chosen, axis=1, keepdims=True)
    def pack(value):
        return jnp.concatenate([value[:, :half_f], value[:, half_f:]], axis=0).astype(BF16)

    take_tokens.wait()
    row = iota((nx * CAP, t_count), 0).astype(F32)
    keys = {}

    def dispatch(n):
        sel = []
        for s in range(n * planes, (n + 1) * planes):
            wanted = jnp.zeros((nx * CAP, t_count), F32)
            for i in range(nx):
                place = code[s * nx + i : s * nx + i + 1, :] + float(i * CAP)
                wanted = jnp.where(row == place, 1.0, wanted)
            sel.append(wanted)
        picked = dot(jnp.concatenate(sel, axis=0).astype(BF16), own_tokens[...])
        for k in range(planes):
            s = n * planes + k
            packed = pack(picked[k * nx * CAP : (k + 1) * nx * CAP])
            if offset(s) == 0:
                fwd[s] = packed
            else:
                fwd_send[s] = packed

    def dispatch_send(n):
        for s in range(n * planes, (n + 1) * planes):
            if offset(s):
                to = at_z(plane(offset(s)))
                keys["fwd", s] = send(fwd_send.at[s], fwd.at[s], to)

    dispatch(0)
    pl.semaphore_wait(barrier, len(peers))
    down_keys = []
    for q in range(1, ng):
        to = lax.rem(g + q, ng)
        columns = pl.ds(pl.multiple_of(to * feat, 128), feat)
        down_keys.append(send(down.at[:, columns], dn.at[g], at_g(to)))
    dispatch_send(0)
    for n in range(1, NQ):
        dispatch(n)
        dispatch_send(n)

    for s in range(nz):
        for i in range(nx):
            line = jnp.broadcast_to(number[s * nx + i : s * nx + i + 1, :], (1, 128))
            plane_send[s, i : i + 1, :] = line
        plane_send[s, nx:8, :] = jnp.zeros((8 - nx, 128), F32)
    for s in range(nz):
        if offset(s) == 0:
            plane_recv[s] = plane_send[s]
        else:
            keys["plane", s] = send(plane_send.at[s], plane_recv.at[s], at_z(plane(offset(s))))
    hist[...] = jnp.zeros_like(hist)

    def swap(a, b):
        row = iota((2 * quarter_rows, 1), 0).astype(F32)
        j, row = split(row, 2 * a * CAP)
        half, row = split(row, a * CAP)
        i, p = split(row, CAP)
        source = i * (2.0 * b * CAP) + half * (b * CAP) + j * CAP + p
        return mask_bf16(iota((2 * quarter_rows, 2 * quarter_rows), 1).astype(F32) == source)

    size = 2 * quarter_rows
    perm_in[...] = swap(planes, nx)
    perm_out[...] = swap(nx, planes)

    def split_weights():
        take_w.wait()
        wide = 2 * 128
        r, q = iota((wide, wide), 0), iota((wide, wide), 1)
        order = mask_bf16(q == jnp.where(r < 128, 2 * r, 2 * (r - 128) + 1))
        per = feat // 128

        @pl.loop(0, ng)
        def _(gg):
            for b in range(per):
                first = pl.multiple_of((gg * per + b) * wide, wide)
                parted = dot(order, w_raw[pl.ds(first, wide)]).astype(BF16)
                half, b = b * 128 // half_f, b * 128 % half_f
                to = 2 * h_local * half
                place = pl.ds(pl.multiple_of(lax.div(gg, NC) * half_f + b, 128), 128)
                w_split[lax.rem(gg, NC), place, to : to + h_local] = parted[:128]
                w_split[lax.rem(gg, NC), place, to + h_local : to + 2 * h_local] = parted[128:]

    def home_weights():
        take_weights.wait()
        eye = mask_f32(iota((t_count, t_count), 0) == iota((t_count, t_count), 1))
        routes_c = dot_nt(eye, routes_v[...].astype(F32), HIGHEST)
        weights_c = dot_nt(eye, weights_v[...], HIGHEST)
        before = mask_bf16(iota((t_count, t_count), 1) < iota((t_count, t_count), 0))
        lane_k, in_plane = split(iota((1, size), 1).astype(F32), back_rows)
        _, entry = split(in_plane, nx * CAP)
        lane_i, place = split(entry, CAP)
        for quarter in range(NQ):
            expert = jnp.full((1, size), -1.0, F32)
            for k in range(planes):
                j = offset(quarter * planes + k)
                for i in range(nx):
                    e = slots[lax.rem(x + i, nx) * nz + plane(j)].astype(F32)
                    expert = jnp.where((lane_k == k) & (lane_i == i), e, expert)
            hit = jnp.zeros((t_count, size), F32)
            weight = hit
            for k in range(picks):
                eq = routes_c[:, k : k + 1] == expert
                hit = jnp.where(eq, 1.0, hit)
                weight = jnp.where(eq, weights_c[:, k : k + 1], weight)
            earlier = dot(before, hit.astype(BF16))
            weight = jnp.where((hit > 0.5) & (earlier == place), weight, 0.0)
            top = weight.astype(BF16)
            weights_hi[quarter] = top
            weights_lo[quarter] = (weight - top.astype(F32)).astype(BF16)

    def select(n):
        for s in range(n * planes, (n + 1) * planes):
            if offset(s):
                arrived(keys["fwd", s], fwd.at[s])
        block = fwd[n * planes : (n + 1) * planes].reshape(size, half_f)
        moved = dot(perm_in[...], block).astype(BF16)
        for i in range(nx):
            part = moved[i * 2 * part_rows : (i + 1) * 2 * part_rows]
            if i == 0:
                rows[g, n, 0] = part
            else:
                xsend[n, i - 1] = part
                keys["x", n, i] = send(
                    xsend.at[n, i - 1], rows.at[g, n, i], at_x(lax.rem(x + i, nx))
                )

    def rows_1(n):
        for i in range(1, nx):
            arrived(keys["x", n, i], rows.at[g, n, i])
        own = rows.at[g, n]
        keys["r_up", n] = send(own, own, at_g(g_up))
        keys["r_dn", n] = send(own, own, at_g(g_dn))
        keys["r_mate", n] = send(own, own, at_g(g_mate))

    near, far = pl.ds(0, nx // 2), pl.ds(nx // 2, nx // 2)

    def rows_2(n):
        ref = rows.at[g_dn, n]
        arrived(keys["r_up", n], ref)
        keys["r_up2", n] = send(rows.at[g_dn, n, near], rows.at[g_dn, n, near], at_g(g_up))
        keys["m_dn", n] = send(ref, ref, at_g(g_mate))
        ref = rows.at[g_up, n]
        arrived(keys["r_dn", n], ref)
        keys["r_dn2", n] = send(rows.at[g_up, n, far], rows.at[g_up, n, far], at_g(g_dn))
        keys["m_up", n] = send(ref, ref, at_g(g_mate))

    def rows_3(n):
        ref = rows.at[g_op, n, near]
        arrived(keys["r_up2", n], ref)
        keys["m_op1", n] = send(ref, ref, at_g(g_mate))
        ref = rows.at[g_op, n, far]
        arrived(keys["r_dn2", n], ref)
        keys["m_op2", n] = send(ref, ref, at_g(g_mate))
        gate_and_up(n, c)

    def rows_4(n):
        arrived(keys["r_mate", n], rows.at[g_mate, n])
        arrived(keys["m_dn", n], rows.at[mate_of(g_dn), n])
        arrived(keys["m_up", n], rows.at[mate_of(g_up), n])
        arrived(keys["m_op1", n], rows.at[mate_of(g_op), n, near])
        arrived(keys["m_op2", n], rows.at[mate_of(g_op), n, far])
        gate_and_up(n, other)
        activate(n)
        own = hid.at[g, n]
        for name, to in (("up", g_up), ("dn", g_dn), ("op", g_op), ("mate", g_mate)):
            keys["h_" + name, n] = send(own, own, at_g(to))

    def hid_2(n):
        for name, src in (("up", g_dn), ("dn", g_up), ("op", g_op)):
            ref = hid.at[src, n]
            arrived(keys["h_" + name, n], ref)
            keys["hm_" + name, n] = send(ref, ref, at_g(g_mate))

    def hid_3(n):
        if n == 0:
            take_down.wait()
            for q in range(1, ng):
                arrived(down_keys[q - 1], dn.at[lax.rem(g + ng - q, ng)])
        arrived(keys["h_mate", n], hid.at[g_mate, n])
        for name, src in (("up", g_dn), ("dn", g_up), ("op", g_op)):
            arrived(keys["hm_" + name, n], hid.at[mate_of(src), n])
        output_rows(n)
        if n == NQ - 1:
            send_threshold()

    def gate_and_up(n, core):
        block = jnp.concatenate(
            [rows[g_of(yy, core), n].reshape(size, half_f) for yy in range(NY)], axis=1
        )
        made = dot(block, w_split[core])
        acc[n] = acc[n] + made if n in begun else made
        begun.append(n)

    begun = []

    def activate(n):
        both = []
        for i in range(nx):
            r = 2 * part_rows * i
            both.append(
                acc[n, r : r + part_rows, : 2 * h_local]
                + acc[n, r + part_rows : r + 2 * part_rows, 2 * h_local :]
            )
        both = jnp.concatenate(both, axis=0)
        gate = both[:, :h_local]
        hid[g, n] = (gate / (1.0 + jnp.exp(-gate)) * both[:, h_local:]).astype(BF16)

    wide = hist.shape[0] // 8

    def histogram(n):
        @pl.loop(0, quarter_rows // (2 * wide))
        def _(step):
            first = pl.multiple_of(step * 2 * wide, 2 * wide)
            level = jnp.abs(hid[g, n, pl.ds(first, 2 * wide)].astype(F32))
            where = jnp.clip(level * (NB / HIST_TOP) - 0.5, 0.0, NB - 1.0)
            lower = jnp.floor(where)
            part = where - lower
            coarse = jnp.floor(lower * (1.0 / 16.0))
            fine = lower - 16.0 * coarse
            eight = iota((8, h_local), 0).astype(F32)
            sixteen = iota((16, h_local), 0).astype(F32)
            sides = []
            for side in range(2):
                left, one, share = [], [], []
                for r in range(side * wide, (side + 1) * wide):
                    left.append(mask_f32(coarse[r : r + 1] == eight))
                    match = fine[r : r + 1] == sixteen
                    one.append(mask_f32(match))
                    share.append(jnp.where(match, part[r : r + 1], 0.0))
                sides.append(
                    (
                        jnp.concatenate(left, axis=0).astype(BF16),
                        jnp.concatenate(one + share, axis=0).astype(BF16),
                    )
                )
            a = jnp.concatenate([sides[0][0], sides[1][0]], axis=1)
            b = jnp.concatenate([sides[0][1], sides[1][1]], axis=1)
            hist[...] += dot_nt(a, b)

    def counts_of():
        m, k = 8 * wide, 16 * wide
        own_row = lax.shift_right_logical(iota((m, k), 0), 3) == lax.shift_right_logical(
            iota((m, k), 1), 4
        )
        fold = mask_f32((iota((k, NB), 0) & 15) == (iota((k, NB), 1) & 15))
        own_bin = (iota((m, NB), 0) & 7) == lax.shift_right_logical(iota((m, NB), 1), 4)

        def bins(table):
            folded = dot(jnp.where(own_row, table, 0.0), fold, HIGHEST)
            return jnp.sum(jnp.where(own_bin, folded, 0.0), axis=0, keepdims=True)

        number = bins(hist[:, :k])
        share = jnp.broadcast_to(bins(hist[:, k:]), (8, NB))
        return jnp.broadcast_to(number, (8, NB)) - share + pltpu.roll(share, 1, 1)

    def output_rows(n):
        full = jnp.concatenate([hid[q, n] for q in range(ng)], axis=1)
        made = dot(full, dn[...].reshape(ng * h_local, feat))
        for i in range(nx):
            packed = pack(made[i * part_rows : (i + 1) * part_rows])
            if i == 0:
                outr[n, 0] = packed
            else:
                outs[n, i - 1] = packed
                keys["out", n, i] = send(
                    outs.at[n, i - 1], outr.at[n, i], at_x(lax.rem(x + nx - i, nx))
                )

    def z_return(n):
        for i in range(1, nx):
            arrived(keys["out", n, i], outr.at[n, i])
        moved = dot(perm_out[...], outr[n].reshape(size, half_f)).astype(BF16)
        for k in range(planes):
            s = n * planes + k
            block = moved[k * back_rows : (k + 1) * back_rows]
            j = offset(s)
            if j == 0:
                zrecv[s] = block
            else:
                zsend[s] = block
                keys["back", s] = send(zsend.at[s], zrecv.at[s], at_z(plane(-j)))

    def combine(n):
        for s in range(n * planes, (n + 1) * planes):
            if offset(s):
                arrived(keys["back", s], zrecv.at[s])
        back = zrecv[n * planes : (n + 1) * planes].reshape(size, half_f)
        _, in_plane = split(iota((1, size), 1).astype(F32), back_rows)
        upper = in_plane < nx * CAP
        zero = jnp.zeros((), BF16)
        for half in range(2):
            keep = upper if half == 0 else jnp.logical_not(upper)
            high = jnp.where(keep, weights_hi[n], zero)
            low = jnp.where(keep, weights_lo[n], zero)
            gained = dot(high, back) + dot(low, back)
            cols = slice(half * half_f, (half + 1) * half_f)
            if n > 0:
                gained = total[:, cols] + gained
            if n < NQ - 1:
                total[:, cols] = gained
            else:
                mixed[:, cols] = gained.astype(BF16)

    def send_valid():
        number = jnp.zeros((8, 128), F32)
        for s in range(nz):
            if offset(s):
                arrived(keys["plane", s], plane_recv.at[s])
            number = number + plane_recv[s]
        for i in range(nx):
            line = jnp.broadcast_to(number[i : i + 1, :], (8, 128))
            if i == 0:
                valid_recv[0] = line
            else:
                valid_send[i - 1] = line
                keys["valid", i] = send(
                    valid_send.at[i - 1], valid_recv.at[i], at_x(lax.rem(x + i, nx))
                )

    def send_counts():
        counts = counts_of()
        filled = valid_recv[0]
        for i in range(1, nx):
            arrived(keys["valid", i], valid_recv.at[i])
            filled = filled + valid_recv[i]
        empty = (float(NQ * quarter_rows) - filled) * float(h_local)
        count_recv[g] = counts - jnp.where(iota((8, NB), 1) == 0, empty, 0.0)
        for q in range(1, ng):
            keys["count", q] = send(count_recv.at[g], count_recv.at[g], at_g(lax.rem(g + q, ng)))

    def send_threshold():
        for q in range(1, ng):
            arrived(keys["count", q], count_recv.at[lax.rem(g + ng - q, ng)])
        counts = count_recv[0]
        for q in range(1, ng):
            counts = counts + count_recv[q]
        sums = jnp.sum(counts, axis=1, keepdims=True)
        below = mask_f32(iota((NB, NB), 0) < iota((NB, NB), 1))
        before_bin = dot(counts, below, HIGHEST)
        fraction = jnp.clip((QUANTILE * sums - before_bin) / jnp.maximum(counts, 1.0), 0.0, 1.0)
        threshold = (HIST_TOP / NB) * jnp.sum(fraction, axis=1, keepdims=True)
        th_send[...] = jnp.broadcast_to(threshold, (8, 128))
        th_recv[0] = th_send[...]
        for j in range(1, nz):
            keys["th", j] = send(th_send, th_recv.at[j], at_z(plane(j)))

    def share_thresholds():
        gathered = jnp.zeros((8, 128), F32)
        for j in range(nz):
            if j:
                arrived(keys["th", j], th_recv.at[j])
            place = x * nz + plane(-j)
            gathered = jnp.where(iota((8, 128), 1) == place, th_recv[j], gathered)
        tx_send[...] = gathered
        for i in range(1, nx):
            keys["tx", i] = send(tx_send, tx_recv.at[i - 1], at_x(lax.rem(x + i, nx)))

    steps = (select, rows_1, rows_2, rows_3, rows_4, histogram, hid_2, hid_3, z_return)
    split_weights()
    home_weights()
    for entry in ORDER:
        if entry == 51:
            send_valid()
        steps[entry // 10](entry % 10)
        if entry == 53:
            send_counts()

    combine(0)
    combine(1)
    share_thresholds()
    combine(2)
    gathered = tx_send[...]
    for i in range(1, nx):
        arrived(keys["tx", i], tx_recv.at[i - 1])
        gathered = gathered + tx_recv[i - 1]
    thresholds[...] = gathered[0:1, : nx * nz]
    for copy in started:
        copy.wait_send()
    combine(3)


def per_device(nx, nz, tokens, routes, route_weights, slots, gate_up, down):
    ng = NY * NC
    t_count, width = tokens.shape
    picks = routes.shape[1]
    feat = width // ng
    half_f = feat // 2
    h_local = down.shape[1]
    part_rows = nz // NQ * CAP
    quarter_rows = nx * part_rows
    back_rows = 2 * nx * CAP
    size = 2 * quarter_rows
    wide = 16 if quarter_rows % 32 == 0 else 2

    vmem = pl.BlockSpec(memory_space=pltpu.VMEM)
    hbm = pl.BlockSpec(memory_space=pl.ANY)
    mixed, thresholds = pl.pallas_call(
        functools.partial(kernel, nx, nz),
        out_shape=(
            jax.ShapeDtypeStruct((t_count, feat), BF16),
            jax.ShapeDtypeStruct((1, slots.shape[0]), F32),
        ),
        in_specs=[hbm] * 6,
        out_specs=(vmem, vmem),
        scratch_shapes=[
            pltpu.SMEM(slots.shape, jnp.int32),
            pltpu.VMEM((picks, t_count), jnp.int32),
            pltpu.VMEM((picks, t_count), F32),
            pltpu.VMEM((t_count, feat), BF16),
            pltpu.VMEM((nz, back_rows, half_f), BF16),
            pltpu.VMEM((nz, back_rows, half_f), BF16),
            pltpu.VMEM((NQ, nx - 1, 2 * part_rows, half_f), BF16),
            pltpu.VMEM((ng, NQ, nx, 2 * part_rows, half_f), BF16),
            pltpu.VMEM((2 * width, h_local), BF16),
            pltpu.VMEM((NC, NY * half_f, 4 * h_local), BF16),
            pltpu.VMEM((ng, h_local, feat), BF16),
            pltpu.VMEM((NQ, size, 4 * h_local), F32),
            pltpu.VMEM((ng, NQ, quarter_rows, h_local), BF16),
            pltpu.VMEM((NQ, nx - 1, 2 * part_rows, half_f), BF16),
            pltpu.VMEM((NQ, nx, 2 * part_rows, half_f), BF16),
            pltpu.VMEM((nz, back_rows, half_f), BF16),
            pltpu.VMEM((nz, back_rows, half_f), BF16),
            pltpu.VMEM((size, size), BF16),
            pltpu.VMEM((size, size), BF16),
            pltpu.VMEM((NQ, t_count, size), BF16),
            pltpu.VMEM((NQ, t_count, size), BF16),
            pltpu.VMEM((t_count, feat), F32),
            pltpu.VMEM((8 * wide, 32 * wide), F32),
            pltpu.VMEM((nz, 8, 128), F32),
            pltpu.VMEM((nz, 8, 128), F32),
            pltpu.VMEM((nx - 1, 8, 128), F32),
            pltpu.VMEM((nx, 8, 128), F32),
            pltpu.VMEM((ng, 8, 128), F32),
            pltpu.VMEM((8, 128), F32),
            pltpu.VMEM((nz, 8, 128), F32),
            pltpu.VMEM((8, 128), F32),
            pltpu.VMEM((nx - 1, 8, 128), F32),
            pltpu.SemaphoreType.DMA((SEMS,)),
            pltpu.SemaphoreType.DMA((SEMS,)),
            pltpu.SemaphoreType.DMA((6,)),
        ],
        compiler_params=pltpu.CompilerParams(
            collective_id=0, has_side_effects=True, vmem_limit_bytes=60 << 20
        ),
        cost_estimate=pl.CostEstimate(
            flops=4 << 30, bytes_accessed=8 << 20, transcendentals=1 << 17
        ),
    )(
        tokens,
        routes.T,
        route_weights.T,
        slots,
        gate_up.reshape(2 * width, h_local),
        down[0],
    )
    return mixed, thresholds.reshape(-1)


def solution(mesh, nx=NX, nz=NZ):
    placed = (
        P("ep", None),
        P("ep", None),
        P("ep", None),
        P(),
        P("ep", None, None, "grp"),
        P("ep", "grp", None),
    )
    return jax.shard_map(
        functools.partial(per_device, nx, nz),
        mesh=mesh,
        in_specs=placed,
        out_specs=(P("ep", "grp"), P()),
        check_vma=False,
    )
```
